32 devices in a mesh: val: 4 (over x, core), cond: 2 (over y), grid: 4 (over z).
Axes of the slice: x: 2, y: 2, z: 4, core: 2. Of those that a mesh axis runs over, the one named last changes fastest.
Arguments:
- valence_orbitals: bfloat16 [16, 96, 9216], P('val', 'grid'), may hold values from -6 to 6
- conduction_orbitals: bfloat16 [8, 96, 9216], P('cond', 'grid'), may hold values from -6 to 6
- valence_energy: float32 [16], replicated, may hold values from -12 to -1
- conduction_energy: float32 [8], replicated, may hold values from 0.5 to 10
- grid_index: int32 [6144], replicated, may hold values from 0 to 884735, as said below
Outputs:
- response: float32 [2, 6144, 6144], P(None, ('val', 'grid'), 'cond')
The draws below stay inside these ranges and needn't reach their ends.
Inputs may be any that keep to these rules, and one draw needn't show every extreme that they name: `grid_index`: distinct flat points of the 96 x 96 x 96 frequency grid.
All inputs are finite; a program needn't handle non-finite values.
Results may differ from the reference program's by a relative error of at most 0.0098.
Values may be sent and summed in bfloat16 or wider, within the bound.
A program may use at most 128 MiB of HBM per device.

```python
import math
import jax
import jax.numpy as jnp
from jax import lax

NGRID = 96
NG = 6144
NV = 16
NC = 8


def draw_grid_index(key, part):
    point_count = NGRID ** 3
    interior = jax.random.permutation(key, point_count - 2)[:NG - 2] + 1
    return jnp.concatenate([jnp.zeros((1,), jnp.int32), interior.astype(jnp.int32), jnp.full((1,), point_count - 1, jnp.int32)])


def level_of(stream_key, extent, shards, least, high):
    factor_of = 1.0
    for dim, shards_of in shards:
        heights = jax.random.uniform(jax.random.fold_in(jax.random.fold_in(stream_key, 6), dim), (shards_of,), jnp.float32, least / len(shards), high / len(shards))
        factor_of = factor_of * jnp.repeat(jnp.exp(heights), extent[dim] // shards_of).reshape((-1,) + (1,) * (len(extent) - 1 - dim))
    return factor_of


def centred(rng, shape, width, most, shards=(), held_as=jnp.bfloat16):
    result = width * jax.random.normal(rng, shape, jnp.float32)
    if shards:
        result = result * level_of(rng, shape, shards, -0.22, 0.18)
    return jnp.clip(result, -most, most).astype(held_as)


def setup_inputs(seed: int = 0) -> dict:
    key_of = jax.random.split(jax.random.key(seed), 6)
    return {
        "valence_orbitals": centred(key_of[0], (NV, NGRID, NGRID * NGRID), 1.0, 6.0, ((0, 4), (1, 4))),
        "conduction_orbitals": centred(key_of[1], (NC, NGRID, NGRID * NGRID), 1.0, 6.0, ((0, 2), (1, 4))),
        "valence_energy": jnp.clip(jax.random.uniform(key_of[2], (NV,), jnp.float32, -12.0, -1.0), -12.0, -1.0),
        "conduction_energy": jnp.clip(jax.random.uniform(key_of[3], (NC,), jnp.float32, 0.5, 10.0), 0.5, 10.0),
        "grid_index": draw_grid_index(jax.random.fold_in(key_of[5], 71), 0),
    }


freq_squared = 4.0

def line_tables(points):
    indices = jnp.arange(points, dtype=jnp.int32)
    phases = indices[:, None] * indices[None, :] % points
    angles = phases.astype(jnp.float32) * (2.0 * math.pi / points)
    return (jnp.cos(angles).astype(jnp.bfloat16), (-jnp.sin(angles)).astype(jnp.bfloat16))

def reference(valence_orbitals, conduction_orbitals, valence_energy, conduction_energy, grid_index):
    line_cos, line_sin = line_tables(NGRID)
    cos_wide = line_cos.astype(jnp.float32)
    sin_wide = line_sin.astype(jnp.float32)
    z_table = jnp.concatenate([line_cos, line_sin], axis=1)
    scale = NGRID ** (-1.5)

    def one_band(orbital):
        products = (orbital.astype(jnp.float32)[None] * conduction_orbitals.astype(jnp.float32)).astype(jnp.bfloat16)
        flat_rows = products.reshape(NC * NGRID * NGRID, NGRID)
        z_part = jnp.dot(flat_rows, z_table, preferred_element_type=jnp.float32).astype(jnp.bfloat16)
        z_part = z_part.reshape(NC, NGRID, NGRID, 2 * NGRID).astype(jnp.float32)
        first = jnp.einsum('cxyk,yp->cxpk', z_part, cos_wide)
        second = jnp.einsum('cxyk,yp->cxpk', z_part, sin_wide)
        plane_real = first[..., :NGRID] - second[..., NGRID:]
        plane_imag = second[..., :NGRID] + first[..., NGRID:]
        plane = jnp.concatenate([plane_real, plane_imag], axis=-1).astype(jnp.bfloat16).astype(jnp.float32)
        first = jnp.einsum('cxpk,xq->cqpk', plane, cos_wide)
        second = jnp.einsum('cxpk,xq->cqpk', plane, sin_wide)
        full_real = (first[..., :NGRID] - second[..., NGRID:]).reshape(NC, NGRID ** 3)
        full_imag = (second[..., :NGRID] + first[..., NGRID:]).reshape(NC, NGRID ** 3)
        picked_real = jnp.take(full_real, grid_index, axis=1) * scale
        picked_imag = jnp.take(full_imag, grid_index, axis=1) * scale
        return jnp.stack([picked_real, picked_imag]).astype(jnp.bfloat16)
    values = lax.map(one_band, valence_orbitals)
    values = jnp.transpose(values, (1, 0, 2, 3)).reshape(2, NV * NC, NG)
    delta = valence_energy[:, None] - conduction_energy[None, :]
    weights = (4.0 * delta / (delta * delta + freq_squared) / math.sqrt(NV * NC)).reshape(NV * NC)
    scaled = (values.astype(jnp.float32) * weights[None, :, None]).astype(jnp.bfloat16)
    real_sum = jnp.dot(scaled[0].T, values[0], preferred_element_type=jnp.float32) + jnp.dot(scaled[1].T, values[1], preferred_element_type=jnp.float32)
    imag_sum = jnp.dot(scaled[1].T, values[0], preferred_element_type=jnp.float32) - jnp.dot(scaled[0].T, values[1], preferred_element_type=jnp.float32)
    return jnp.stack([real_sum, imag_sum])
```

```python
import functools
import math

import jax
import jax.numpy as jnp
import numpy as np
from jax import lax
from jax.experimental import pallas as pl
from jax.experimental.pallas import tpu as pltpu
from jax.sharding import PartitionSpec as P

freq_squared = 4.0
LANES = 128


def line_tables(points):
    indices = jnp.arange(points, dtype=jnp.int32)
    phases = indices[:, None] * indices[None, :] % points
    angles = phases.astype(jnp.float32) * (2.0 * math.pi / points)
    return (jnp.cos(angles).astype(jnp.bfloat16), (-jnp.sin(angles)).astype(jnp.bfloat16))


def spectra_kernel(
    points, half, half_pad, bands, unroll,
    row_ref, line_ref, valence_ref, conduction_ref, spread_ref, z_ref, y_ref, cos_ref, sin_ref,
    fold_ref, out_ref, planes, picked,
):
    pitch = points + 1
    chunk = half * pitch
    parts = 2 * bands

    def z_pass(y):
        rows = pl.ds(pl.multiple_of(y * points, points), points)
        wide = jnp.dot(valence_ref[rows, :], spread_ref[...], preferred_element_type=jnp.float32)
        other = conduction_ref[rows, :].astype(jnp.float32)
        products = (wide * jnp.concatenate([other] * bands, axis=1)).astype(jnp.bfloat16)
        result = jnp.dot(z_ref[...], products, preferred_element_type=jnp.float32)
        for part in range(parts):
            kind, band = part // bands, part % bands
            planes[pl.ds(part * chunk + y, half, stride=pitch), :] = result[
                kind * half_pad : kind * half_pad + half, band * LANES : (band + 1) * LANES
            ]

    def y_pass(q):
        slabs = [planes[pl.ds(part * chunk + q * pitch, points), :] for part in range(parts)]
        block = jnp.concatenate(
            [jnp.concatenate(slabs[kind * bands : (kind + 1) * bands], axis=1) for kind in range(2)],
            axis=0,
        ).astype(jnp.bfloat16)
        result = jnp.dot(y_ref[...], block, preferred_element_type=jnp.float32)
        for part in range(parts):
            kind, band = part // bands, part % bands
            planes[pl.ds(part * chunk + q * pitch, points), :] = result[
                kind * points : (kind + 1) * points, band * LANES : (band + 1) * LANES
            ]

    def pick(block):
        def some(step, carry):
            for inner in range(unroll):
                place = step * unroll + inner
                vector = block * LANES + place
                line = line_ref[vector]
                values = planes[pl.ds(row_ref[vector], parts, stride=chunk), :]
                swapped = pltpu.roll(values, bands, axis=0)
                picked[pl.ds(place, parts, stride=LANES + 1), :] = (
                    values * cos_ref[line] + swapped * sin_ref[line]
                )
            return carry

        lax.fori_loop(0, LANES // unroll, some, 0)
        rows = jnp.concatenate(
            [
                picked[part * (LANES + 1) : part * (LANES + 1) + LANES, :].astype(jnp.bfloat16)
                for part in range(parts)
            ],
            axis=1,
        )
        folded = jnp.dot(rows, fold_ref[...], preferred_element_type=jnp.float32)
        out_ref[:, pl.ds(pl.multiple_of(block * LANES, LANES), LANES)] = folded.T[
            : out_ref.shape[0], :
        ].astype(out_ref.dtype)

    def loop(count, body, step):
        def several(index, carry):
            for inner in range(step):
                body(index * step + inner)
            return carry

        lax.fori_loop(0, count // step, several, 0)
        for rest in range(count - count % step, count):
            body(rest)

    loop(points, z_pass, 2)
    loop(half, y_pass, 2)
    loop(out_ref.shape[1] // LANES, pick, 1)


def partial_spectra(valence, conduction, grid_index):
    bands, depth, plane = valence.shape
    conduction_bands = conduction.shape[0]
    points = depth * lax.axis_size("grid")
    half = points // 2 + 1
    half_pad = -(-half // 16) * 16
    used = conduction_bands * depth
    parts = 2 * bands
    vectors = grid_index.shape[0]
    line_cos, line_sin = line_tables(points)

    spread = np.zeros((bands * depth, bands, LANES), np.float32)
    for band in range(bands):
        for other in range(conduction_bands):
            for x in range(depth):
                spread[band * depth + x, band, other * depth + x] = 1.0
    spread = jnp.asarray(spread.reshape(bands * depth, bands * LANES), jnp.bfloat16)
    columns = parts * conduction_bands
    fold = np.zeros((parts, LANES, LANES), np.float32)
    for part in range(parts):
        for other in range(conduction_bands):
            fold[part, other * depth : (other + 1) * depth, part * conduction_bands + other] = 1.0
    fold = jnp.asarray(fold.reshape(parts * LANES, LANES), jnp.bfloat16)

    z_table = jnp.zeros((2 * half_pad, points), jnp.bfloat16)
    z_table = z_table.at[:half].set(line_cos.T[:half])
    z_table = z_table.at[half_pad : half_pad + half].set(line_sin.T[:half])
    y_table = jnp.concatenate(
        [
            jnp.concatenate([line_cos.T, -line_sin.T], axis=1),
            jnp.concatenate([line_sin.T, line_cos.T], axis=1),
        ],
        axis=0,
    )

    scale = points ** (-1.5)
    offset = lax.axis_index("grid") * depth
    def lanes_of(table):
        local = lax.dynamic_slice_in_dim(table.T.astype(jnp.float32) * scale, offset, depth, 1)
        return jnp.pad(jnp.tile(local, (1, conduction_bands)), ((0, 0), (0, LANES - used)))

    cos_lanes = lanes_of(line_cos)
    sin_lanes = lanes_of(line_sin)
    upper = (jnp.arange(parts) < bands)[None, :, None]
    cos_rows = jnp.broadcast_to(cos_lanes[:, None, :], (points, parts, LANES))
    sin_rows = jnp.broadcast_to(sin_lanes[:, None, :], (points, parts, LANES))
    cos_table = jnp.concatenate([cos_rows, jnp.where(upper, cos_rows, -cos_rows)], axis=0)
    sin_table = jnp.concatenate([jnp.where(upper, -sin_rows, sin_rows), -sin_rows], axis=0)

    line = grid_index // (points * points)
    remainder = grid_index % (points * points)
    row = remainder // points
    column = remainder % points
    mirrored = column >= half
    line = jnp.where(mirrored, points + (points - line) % points, line)
    row = jnp.where(mirrored, (points - row) % points, row)
    column = jnp.where(mirrored, points - column, column)
    place = column * (points + 1) + row

    valence_points = valence.reshape(bands * depth, plane).T
    conduction_points = jnp.pad(conduction.reshape(used, plane).T, ((0, 0), (0, LANES - used)))
    vmem = pl.BlockSpec(memory_space=pltpu.VMEM)
    smem = pl.BlockSpec(memory_space=pltpu.SMEM)
    return pl.pallas_call(
        functools.partial(spectra_kernel, points, half, half_pad, bands, 16),
        out_shape=jax.ShapeDtypeStruct((columns, vectors), jnp.bfloat16),
        in_specs=[smem, smem] + [vmem] * 8,
        out_specs=vmem,
        scratch_shapes=[
            pltpu.VMEM((parts * half * (points + 1), LANES), jnp.float32),
            pltpu.VMEM((parts * (LANES + 1), LANES), jnp.float32),
        ],
        compiler_params=pltpu.CompilerParams(vmem_limit_bytes=48 * 2**20),
        name="spectra",
    )(
        place, line, valence_points, conduction_points, spread, z_table, y_table, cos_table,
        sin_table, fold,
    )


def local(valence_orbitals, conduction_orbitals, valence_energy, conduction_energy, grid_index):
    valence_groups = lax.axis_size("val")
    conduction_groups = lax.axis_size("cond")
    grid_groups = lax.axis_size("grid")
    valence_local = valence_orbitals.shape[0]
    conduction_local = conduction_orbitals.shape[0]
    pair_count = valence_local * conduction_local
    vectors = grid_index.shape[0]
    row_width = vectors // (valence_groups * grid_groups)
    column_width = vectors // conduction_groups
    partial = partial_spectra(valence_orbitals, conduction_orbitals, grid_index)
    split = partial.reshape(2 * pair_count, valence_groups, grid_groups, row_width)
    arrived = lax.all_to_all(split, "grid", split_axis=2, concat_axis=2, tiled=True)
    own = jnp.sum(arrived.astype(jnp.float32), axis=2).astype(jnp.bfloat16)
    everything = lax.all_gather(own, ("val", "cond"), axis=0, tiled=False)
    groups = valence_groups * conduction_groups
    rows = lax.dynamic_index_in_dim(everything, lax.axis_index("val"), 2, keepdims=False)
    rows = rows.reshape(groups, 2, pair_count, row_width)
    blocks = valence_groups // conduction_groups if valence_groups % conduction_groups == 0 else 0
    if blocks:
        half = lax.dynamic_slice_in_dim(everything, lax.axis_index("cond") * blocks, blocks, 2)
        columns = lax.all_gather(half, "grid", axis=3, tiled=False)
    else:
        columns = lax.all_gather(everything, "grid", axis=3, tiled=False)
        columns = columns.reshape(groups, 2 * pair_count, vectors)
        columns = lax.dynamic_slice_in_dim(
            columns, lax.axis_index("cond") * column_width, column_width, 2
        )
    columns = columns.reshape(groups * 2 * pair_count, column_width)

    delta = valence_energy[:, None] - conduction_energy[None, :]
    all_pairs = valence_energy.shape[0] * conduction_energy.shape[0]
    weights = 4.0 * delta / (delta * delta + freq_squared) / math.sqrt(all_pairs)
    weights = weights.reshape(valence_groups, valence_local, conduction_groups, conduction_local)
    weights = jnp.transpose(weights, (0, 2, 1, 3)).reshape(groups, 1, pair_count, 1)
    scaled = (rows.astype(jnp.float32) * weights).astype(jnp.bfloat16)
    turned = jnp.stack([scaled[:, 1], -scaled[:, 0]], axis=1)
    both = jnp.stack([scaled, turned], axis=0).reshape(2, groups * 2 * pair_count, row_width)
    return lax.dot_general(
        both, columns, (((1,), (0,)), ((), ())), preferred_element_type=jnp.float32
    )


def solution(mesh):
    return jax.shard_map(
        local,
        mesh=mesh,
        in_specs=(P("val", "grid", None), P("cond", "grid", None), P(), P(), P()),
        out_specs=P(None, ("val", "grid"), "cond"),
        check_vma=False,
    )
```

```python
import functools
import math

import jax
import jax.numpy as jnp
import numpy as np
from jax import lax
from jax.experimental import pallas as pl
from jax.experimental.pallas import tpu as pltpu
from jax.sharding import PartitionSpec as P

freq_squared = 4.0
LANES = 128


def line_tables(points):
    indices = jnp.arange(points, dtype=jnp.int32)
    phases = indices[:, None] * indices[None, :] % points
    angles = phases.astype(jnp.float32) * (2.0 * math.pi / points)
    return (jnp.cos(angles).astype(jnp.bfloat16), (-jnp.sin(angles)).astype(jnp.bfloat16))


def spectra_kernel(
    points, half, half_pad, bands, unroll,
    row_ref, line_ref, valence_ref, conduction_ref, spread_ref, z_ref, y_ref, cos_ref, sin_ref,
    fold_ref, out_ref, planes, picked,
):
    pitch = points + 1
    chunk = half * pitch
    parts = 2 * bands

    def z_pass(y):
        rows = pl.ds(pl.multiple_of(y * points, points), points)
        wide = jnp.dot(valence_ref[rows, :], spread_ref[...], preferred_element_type=jnp.float32)
        other = conduction_ref[rows, :].astype(jnp.float32)
        products = (wide * jnp.concatenate([other] * bands, axis=1)).astype(jnp.bfloat16)
        result = jnp.dot(z_ref[...], products, preferred_element_type=jnp.float32)
        for part in range(parts):
            kind, band = part // bands, part % bands
            planes[pl.ds(part * chunk + y, half, stride=pitch), :] = result[
                kind * half_pad : kind * half_pad + half, band * LANES : (band + 1) * LANES
            ]

    def y_pass(q):
        slabs = [planes[pl.ds(part * chunk + q * pitch, points), :] for part in range(parts)]
        block = jnp.concatenate(
            [jnp.concatenate(slabs[kind * bands : (kind + 1) * bands], axis=1) for kind in range(2)],
            axis=0,
        ).astype(jnp.bfloat16)
        result = jnp.dot(y_ref[...], block, preferred_element_type=jnp.float32)
        for part in range(parts):
            kind, band = part // bands, part % bands
            planes[pl.ds(part * chunk + q * pitch, points), :] = result[
                kind * points : (kind + 1) * points, band * LANES : (band + 1) * LANES
            ]

    def pick(block):
        def some(step, carry):
            for inner in range(unroll):
                place = step * unroll + inner
                vector = block * LANES + place
                line = line_ref[vector]
                values = planes[pl.ds(row_ref[vector], parts, stride=chunk), :]
                swapped = pltpu.roll(values, bands, axis=0)
                picked[pl.ds(place, parts, stride=LANES + 1), :] = (
                    values * cos_ref[line] + swapped * sin_ref[line]
                )
            return carry

        lax.fori_loop(0, LANES // unroll, some, 0)
        rows = jnp.concatenate(
            [
                picked[part * (LANES + 1) : part * (LANES + 1) + LANES, :].astype(jnp.bfloat16)
                for part in range(parts)
            ],
            axis=1,
        )
        folded = jnp.dot(rows, fold_ref[...], preferred_element_type=jnp.float32)
        tiles = out_ref.shape[3] // LANES
        tile = block // tiles
        out_ref[
            tile % out_ref.shape[0],
            tile // out_ref.shape[0],
            :,
            pl.ds(pl.multiple_of(block % tiles * LANES, LANES), LANES),
        ] = folded.T[: out_ref.shape[2], :].astype(out_ref.dtype)

    def loop(count, body, step):
        def several(index, carry):
            for inner in range(step):
                body(index * step + inner)
            return carry

        lax.fori_loop(0, count // step, several, 0)
        for rest in range(count - count % step, count):
            body(rest)

    loop(points, z_pass, 2)
    loop(half, y_pass, 2)
    loop(line_ref.shape[0] // LANES, pick, 1)


def partial_spectra(valence, conduction, grid_index):
    valence_groups = lax.axis_size("val")
    grid_groups = lax.axis_size("grid")
    bands, depth, plane = valence.shape
    conduction_bands = conduction.shape[0]
    points = depth * lax.axis_size("grid")
    half = points // 2 + 1
    half_pad = -(-half // 16) * 16
    used = conduction_bands * depth
    parts = 2 * bands
    vectors = grid_index.shape[0]
    line_cos, line_sin = line_tables(points)

    spread = np.zeros((bands * depth, bands, LANES), np.float32)
    for band in range(bands):
        for other in range(conduction_bands):
            for x in range(depth):
                spread[band * depth + x, band, other * depth + x] = 1.0
    spread = jnp.asarray(spread.reshape(bands * depth, bands * LANES), jnp.bfloat16)
    columns = parts * conduction_bands
    fold = np.zeros((parts, LANES, LANES), np.float32)
    for part in range(parts):
        for other in range(conduction_bands):
            fold[part, other * depth : (other + 1) * depth, part * conduction_bands + other] = 1.0
    fold = jnp.asarray(fold.reshape(parts * LANES, LANES), jnp.bfloat16)

    z_table = jnp.zeros((2 * half_pad, points), jnp.bfloat16)
    z_table = z_table.at[:half].set(line_cos.T[:half])
    z_table = z_table.at[half_pad : half_pad + half].set(line_sin.T[:half])
    y_table = jnp.concatenate(
        [
            jnp.concatenate([line_cos.T, -line_sin.T], axis=1),
            jnp.concatenate([line_sin.T, line_cos.T], axis=1),
        ],
        axis=0,
    )

    scale = points ** (-1.5)
    offset = lax.axis_index("grid") * depth
    def lanes_of(table):
        local = lax.dynamic_slice_in_dim(table.T.astype(jnp.float32) * scale, offset, depth, 1)
        return jnp.pad(jnp.tile(local, (1, conduction_bands)), ((0, 0), (0, LANES - used)))

    cos_lanes = lanes_of(line_cos)
    sin_lanes = lanes_of(line_sin)
    upper = (jnp.arange(parts) < bands)[None, :, None]
    cos_rows = jnp.broadcast_to(cos_lanes[:, None, :], (points, parts, LANES))
    sin_rows = jnp.broadcast_to(sin_lanes[:, None, :], (points, parts, LANES))
    cos_table = jnp.concatenate([cos_rows, jnp.where(upper, cos_rows, -cos_rows)], axis=0)
    sin_table = jnp.concatenate([jnp.where(upper, -sin_rows, sin_rows), -sin_rows], axis=0)

    line = grid_index // (points * points)
    remainder = grid_index % (points * points)
    row = remainder // points
    column = remainder % points
    mirrored = column >= half
    line = jnp.where(mirrored, points + (points - line) % points, line)
    row = jnp.where(mirrored, (points - row) % points, row)
    column = jnp.where(mirrored, points - column, column)
    place = column * (points + 1) + row

    valence_points = valence.reshape(bands * depth, plane).T
    conduction_points = jnp.pad(conduction.reshape(used, plane).T, ((0, 0), (0, LANES - used)))
    vmem = pl.BlockSpec(memory_space=pltpu.VMEM)
    smem = pl.BlockSpec(memory_space=pltpu.SMEM)
    return pl.pallas_call(
        functools.partial(spectra_kernel, points, half, half_pad, bands, 16),
        out_shape=jax.ShapeDtypeStruct(
            (grid_groups, valence_groups, columns, vectors // (grid_groups * valence_groups)),
            jnp.bfloat16,
        ),
        in_specs=[smem, smem] + [vmem] * 8,
        out_specs=vmem,
        scratch_shapes=[
            pltpu.VMEM((parts * half * (points + 1), LANES), jnp.float32),
            pltpu.VMEM((parts * (LANES + 1), LANES), jnp.float32),
        ],
        compiler_params=pltpu.CompilerParams(vmem_limit_bytes=48 * 2**20),
        name="spectra",
    )(
        place, line, valence_points, conduction_points, spread, z_table, y_table, cos_table,
        sin_table, fold,
    )


def exchange_kernel(
    part_ref, columns_ref, rows_ref, inbox, own, rs_send, rs_recv, row_send, row_recv, cond_send,
    cond_recv, grid_send, piece_recv, val_send, core_send,
):
    val_size, cond_size, grid_size = (lax.axis_size(name) for name in ("val", "cond", "grid"))
    val, cond, grid = (lax.axis_index(name) for name in ("val", "cond", "grid"))
    blocks = columns_ref.shape[3]
    group = val * cond_size + cond
    sibling = val + 1 - 2 * (val % 2)
    others = [(val + 2 * step) % val_size for step in range(1, val_size // 2)]
    grid_peers = [(grid + step) % grid_size for step in range(1, grid_size)]
    cond_peers = [(cond + step) % cond_size for step in range(1, cond_size)]
    group_size = val_size * cond_size
    group_peers = [(group + step) % group_size for step in range(1, group_size)]

    def copy(source, target, send, receive, device):
        return pltpu.make_async_remote_copy(
            src_ref=source, dst_ref=target, send_sem=send, recv_sem=receive, device_id=device,
            device_id_type=pl.DeviceIdType.MESH,
        )

    barrier = pltpu.get_barrier_semaphore()
    for peer in grid_peers:
        pl.semaphore_signal(
            barrier, inc=1, device_id=(val, cond, peer), device_id_type=pl.DeviceIdType.MESH
        )
    for peer in group_peers:
        pl.semaphore_signal(
            barrier, inc=1, device_id=(peer // cond_size, peer % cond_size, grid),
            device_id_type=pl.DeviceIdType.MESH,
        )
    pl.semaphore_wait(barrier, len(grid_peers) + len(group_peers))

    sent = []
    for step, peer in enumerate(grid_peers):
        sent.append(
            copy(
                part_ref.at[peer], inbox.at[step], rs_send.at[step], rs_recv.at[step],
                (val, cond, peer),
            )
        )
        sent[-1].start()
    for piece in sent:
        piece.wait_recv()
    for block in range(own.shape[0]):
        total = part_ref[grid, block].astype(jnp.float32)
        for step in range(grid_size - 1):
            total = total + inbox[step, block].astype(jnp.float32)
        own[block] = total.astype(own.dtype)

    cond_copies = []
    for step, peer in enumerate(cond_peers):
        cond_copies.append(
            copy(
                own.at[pl.ds(peer * blocks, blocks)], columns_ref.at[grid, val, cond],
                cond_send.at[step], cond_recv.at[step], (val, peer, grid),
            )
        )
        cond_copies[-1].start()
    columns_ref[grid, val, cond] = own[pl.ds(cond * blocks, blocks)]
    rows_ref[val, cond] = own[val]
    for piece in cond_copies:
        piece.wait_recv()
    sent += cond_copies

    def piece_copy(where, source_val, send, device):
        return copy(
            columns_ref.at[where, source_val], columns_ref.at[where, source_val], send,
            piece_recv.at[source_val * grid_size + where], device,
        )

    def spread(where, slot):
        for index, peer in enumerate(others):
            piece = piece_copy(
                where, val, val_send.at[index * grid_size + slot], (peer, cond, grid)
            )
            piece.start()
            sent.append(piece)
        forward(where, val, slot)

    def forward(where, source_val, slot):
        piece = piece_copy(where, source_val, core_send.at[slot], (sibling, cond, grid))
        piece.start()
        sent.append(piece)

    def arrive(where, source_val):
        piece_copy(where, source_val, core_send.at[0], (sibling, cond, grid)).wait_recv()

    for step, peer in enumerate(grid_peers):
        piece = piece_copy(grid, val, grid_send.at[step], (val, cond, peer))
        piece.start()
        sent.append(piece)
    spread(grid, 0)
    row_copies = []
    for step, peer in enumerate(group_peers):
        row_copies.append(
            copy(
                own.at[peer // cond_size], rows_ref.at[val, cond], row_send.at[step],
                row_recv.at[step], (peer // cond_size, peer % cond_size, grid),
            )
        )
        row_copies[-1].start()

    order = [0] + sorted(range(1, grid_size), key=lambda step: min(step, grid_size - step))
    places = [(grid + step) % grid_size for step in order]
    for slot in range(1, grid_size + 1):
        if slot < grid_size:
            arrive(places[slot], val)
            spread(places[slot], slot)
        for index, peer in enumerate(others):
            arrive(places[slot - 1], peer)
            forward(places[slot - 1], peer, grid_size * (index + 1) + slot - 1)
    for where in places:
        for source in [sibling] + [(sibling + 2 * step) % val_size for step in range(1, val_size // 2)]:
            arrive(where, source)
    for step, peer in enumerate(group_peers):
        source = (group + group_size - 1 - step) % group_size
        copy(
            own.at[0], rows_ref.at[source // cond_size, source % cond_size], row_send.at[step],
            row_recv.at[step], (peer // cond_size, peer % cond_size, grid),
        ).wait_recv()
    for piece in sent + row_copies:
        piece.wait_send()


def exchange(partial):
    val_size, cond_size, grid_size = (lax.axis_size(name) for name in ("val", "cond", "grid"))
    columns, width = partial.shape[2:]
    blocks = val_size // cond_size
    vmem = pl.BlockSpec(memory_space=pltpu.VMEM)
    kind = partial.dtype
    dma = pltpu.SemaphoreType.DMA
    return pl.pallas_call(
        exchange_kernel,
        out_shape=[
            jax.ShapeDtypeStruct((grid_size, val_size, cond_size, blocks, columns, width), kind),
            jax.ShapeDtypeStruct((val_size, cond_size, columns, width), kind),
        ],
        in_specs=[vmem],
        out_specs=[vmem, vmem],
        scratch_shapes=[
            pltpu.VMEM((grid_size - 1, val_size, columns, width), kind),
            pltpu.VMEM((val_size, columns, width), kind),
            dma((grid_size - 1,)),
            dma((grid_size - 1,)),
            dma((val_size * cond_size,)),
            dma((val_size * cond_size,)),
            dma((cond_size,)),
            dma((cond_size,)),
            dma((grid_size,)),
            dma((val_size * grid_size,)),
            dma((val_size * grid_size,)),
            dma((val_size * grid_size,)),
        ],
        compiler_params=pltpu.CompilerParams(
            collective_id=0, has_side_effects=True, vmem_limit_bytes=16 * 2**20
        ),
        name="exchange",
    )(partial)


def response_kernel(rows_ref, weights_ref, columns_ref, out_ref, left):
    depth = rows_ref.shape[0]
    width = rows_ref.shape[1]
    height = columns_ref.shape[-2]

    @pl.when((pl.program_id(0) == 0) & (pl.program_id(1) == 0))
    def scale_rows():
        scaled = rows_ref[...].astype(jnp.float32) * weights_ref[:, :1]
        pairs = scaled.reshape(-1, 2, height // 2, width)
        turned = jnp.concatenate([pairs[:, 1:], -pairs[:, :1]], axis=1).reshape(depth, width)
        left[:width] = scaled.T.astype(left.dtype)
        left[width:] = turned.T.astype(left.dtype)

    right = columns_ref[...].reshape(depth, columns_ref.shape[-1])
    out_ref[...] = jnp.dot(left[...], right, preferred_element_type=jnp.float32).reshape(
        out_ref.shape
    )


def response(rows, columns, weights):
    grid_size, val_size, cond_size, blocks, height, width = columns.shape
    depth = val_size * cond_size * height
    return pl.pallas_call(
        response_kernel,
        out_shape=jax.ShapeDtypeStruct((2, width, blocks * grid_size * width), jnp.float32),
        grid=(blocks, grid_size),
        in_specs=[
            pl.BlockSpec((depth, width), lambda block, place: (0, 0)),
            pl.BlockSpec((depth, LANES), lambda block, place: (0, 0)),
            pl.BlockSpec(
                (None, val_size, cond_size, None, height, width),
                lambda block, place: (place, 0, 0, block, 0, 0),
            ),
        ],
        out_specs=pl.BlockSpec(
            (2, width, width), lambda block, place: (0, 0, block * grid_size + place)
        ),
        scratch_shapes=[pltpu.VMEM((2 * width, depth), jnp.bfloat16)],
        compiler_params=pltpu.CompilerParams(vmem_limit_bytes=24 * 2**20),
        name="response",
    )(rows, weights, columns)


def local(valence_orbitals, conduction_orbitals, valence_energy, conduction_energy, grid_index):
    valence_groups = lax.axis_size("val")
    conduction_groups = lax.axis_size("cond")
    grid_groups = lax.axis_size("grid")
    valence_local = valence_orbitals.shape[0]
    conduction_local = conduction_orbitals.shape[0]
    pair_count = valence_local * conduction_local
    vectors = grid_index.shape[0]
    row_width = vectors // (valence_groups * grid_groups)
    column_width = vectors // conduction_groups
    groups = valence_groups * conduction_groups
    depth = groups * 2 * pair_count

    delta = valence_energy[:, None] - conduction_energy[None, :]
    all_pairs = valence_energy.shape[0] * conduction_energy.shape[0]
    weights = 4.0 * delta / (delta * delta + freq_squared) / math.sqrt(all_pairs)
    weights = weights.reshape(valence_groups, valence_local, conduction_groups, conduction_local)
    weights = jnp.transpose(weights, (0, 2, 1, 3)).reshape(groups, 1, pair_count, 1)

    partial = partial_spectra(valence_orbitals, conduction_orbitals, grid_index)
    if valence_groups % 2 == 0 and valence_groups % conduction_groups == 0 and grid_groups > 1:
        columns, rows = exchange(partial)
        spread = jnp.broadcast_to(weights, (groups, 2, pair_count, LANES)).reshape(depth, LANES)
        return response(rows.reshape(depth, row_width), columns, spread)

    arrived = lax.all_to_all(partial, "grid", split_axis=0, concat_axis=0, tiled=True)
    own = jnp.sum(arrived.astype(jnp.float32), axis=0).astype(jnp.bfloat16)
    everything = lax.all_gather(own, ("val", "cond"), axis=0, tiled=False)
    rows = lax.dynamic_index_in_dim(everything, lax.axis_index("val"), 1, keepdims=False)
    rows = rows.reshape(groups, 2, pair_count, row_width)
    columns = lax.all_gather(jnp.swapaxes(everything, 1, 2), "grid", axis=3, tiled=False)
    columns = lax.dynamic_slice_in_dim(
        columns.reshape(depth, vectors), lax.axis_index("cond") * column_width, column_width, 1
    )
    scaled = (rows.astype(jnp.float32) * weights).astype(jnp.bfloat16)
    turned = jnp.stack([scaled[:, 1], -scaled[:, 0]], axis=1)
    both = jnp.stack([scaled, turned], axis=0).reshape(2, depth, row_width)
    return lax.dot_general(
        both, columns, (((1,), (0,)), ((), ())), preferred_element_type=jnp.float32
    )


def solution(mesh):
    return jax.shard_map(
        local,
        mesh=mesh,
        in_specs=(P("val", "grid", None), P("cond", "grid", None), P(), P(), P()),
        out_specs=P(None, ("val", "grid"), "cond"),
        check_vma=False,
    )
```

```python
import functools
import math

import jax
import jax.numpy as jnp
import numpy as np
from jax import lax
from jax.experimental import pallas as pl
from jax.experimental.pallas import tpu as pltpu
from jax.sharding import PartitionSpec as P

freq_squared = 4.0
LANES = 128
SUBLANES = 8


def line_tables(points):
    indices = jnp.arange(points, dtype=jnp.int32)
    phases = indices[:, None] * indices[None, :] % points
    angles = phases.astype(jnp.float32) * (2.0 * math.pi / points)
    return (jnp.cos(angles).astype(jnp.bfloat16), (-jnp.sin(angles)).astype(jnp.bfloat16))


def spectra_kernel(
    points, half, half_pad, bands, unroll,
    row_ref, line_ref, valence_ref, conduction_ref, spread_ref, z_ref, y_ref, cos_ref, sin_ref,
    fold_ref, out_ref, lines, planes, picked,
):
    parts = 2 * bands
    groups = points // SUBLANES
    pitch = SUBLANES + 1
    depth = valence_ref.shape[1]
    used = conduction_ref.shape[0] * depth
    width = out_ref.shape[3]

    def z_pass(group):
        span = SUBLANES * points
        place = pl.ds(pl.multiple_of(group * span, LANES), span)
        valence = valence_ref[:, :, place].astype(jnp.float32).reshape(bands * depth, span)
        conduction = conduction_ref[:, :, place].astype(jnp.float32).reshape(used, span)
        if used < LANES:
            conduction = jnp.concatenate(
                [conduction, jnp.zeros((LANES - used, span), jnp.float32)], axis=0
            )
        wide = jnp.dot(
            valence.T.astype(jnp.bfloat16), spread_ref[...], preferred_element_type=jnp.float32
        )
        products = (wide * jnp.concatenate([conduction.T] * bands, axis=1)).astype(jnp.bfloat16)
        for inner in range(SUBLANES):
            result = jnp.dot(
                z_ref[...],
                products[inner * points : (inner + 1) * points],
                preferred_element_type=jnp.float32,
            )
            for part in range(parts):
                kind, band = part // bands, part % bands
                start = (part * groups + group) * half * pitch + inner
                lines[pl.ds(start, half, stride=pitch), :] = result[
                    kind * half_pad : kind * half_pad + half, band * LANES : (band + 1) * LANES
                ]

    def y_pass(q):
        def slab(part):
            return jnp.concatenate(
                [
                    lines[pl.ds(((part * groups + group) * half + q) * pitch, SUBLANES), :]
                    for group in range(groups)
                ],
                axis=0,
            )

        block = jnp.concatenate(
            [
                jnp.concatenate([slab(kind * bands + band) for band in range(bands)], axis=1)
                for kind in range(2)
            ],
            axis=0,
        ).astype(jnp.bfloat16)
        result = jnp.dot(y_ref[...], block, preferred_element_type=jnp.float32)
        for part in range(parts):
            kind, band = part // bands, part % bands
            planes[pl.ds(q * points * pitch + part, points, stride=pitch), :] = result[
                kind * points : (kind + 1) * points, band * LANES : (band + 1) * LANES
            ]

    def pick(tile):
        def some(step, carry):
            found = []
            for inner in range(unroll):
                vector = tile * width + step * unroll + inner
                line = line_ref[vector]
                values = planes[pl.ds(row_ref[vector], parts), :]
                swapped = pltpu.roll(values, bands, axis=0)
                found.append(values * cos_ref[line] + swapped * sin_ref[line])
            for inner in range(unroll):
                picked[pl.ds((step * unroll + inner) * pitch, parts), :] = found[inner]
            return carry

        lax.fori_loop(0, width // unroll, some, 0)
        rows = jnp.concatenate(
            [picked[pl.ds(part, width, stride=pitch), :].astype(jnp.bfloat16) for part in range(parts)],
            axis=1,
        )
        folded = jnp.dot(rows, fold_ref[...], preferred_element_type=jnp.float32)
        out_ref[tile % out_ref.shape[0], tile // out_ref.shape[0]] = folded.T[
            : out_ref.shape[2], :
        ].astype(out_ref.dtype)

    def loop(count, body, step):
        def several(index, carry):
            for inner in range(step):
                body(index * step + inner)
            return carry

        lax.fori_loop(0, count // step, several, 0)
        for rest in range(count - count % step, count):
            body(rest)

    loop(groups, z_pass, 1)
    loop(half, y_pass, 4)
    loop(line_ref.shape[0] // width, pick, 1)


def partial_spectra(valence, conduction, grid_index):
    valence_groups = lax.axis_size("val")
    grid_groups = lax.axis_size("grid")
    bands, depth, plane = valence.shape
    conduction_bands = conduction.shape[0]
    points = depth * lax.axis_size("grid")
    half = points // 2 + 1
    half_pad = -(-half // 16) * 16
    used = conduction_bands * depth
    parts = 2 * bands
    vectors = grid_index.shape[0]
    width = vectors // (grid_groups * valence_groups)
    line_cos, line_sin = line_tables(points)

    spread = np.zeros((bands * depth, bands, LANES), np.float32)
    for band in range(bands):
        for other in range(conduction_bands):
            for x in range(depth):
                spread[band * depth + x, band, other * depth + x] = 1.0
    spread = jnp.asarray(spread.reshape(bands * depth, bands * LANES), jnp.bfloat16)
    columns = parts * conduction_bands
    fold = np.zeros((parts, LANES, LANES), np.float32)
    for part in range(parts):
        for other in range(conduction_bands):
            fold[part, other * depth : (other + 1) * depth, part * conduction_bands + other] = 1.0
    fold = jnp.asarray(fold.reshape(parts * LANES, LANES), jnp.bfloat16)

    z_table = jnp.zeros((2 * half_pad, points), jnp.bfloat16)
    z_table = z_table.at[:half].set(line_cos.T[:half])
    z_table = z_table.at[half_pad : half_pad + half].set(line_sin.T[:half])
    y_table = jnp.concatenate(
        [
            jnp.concatenate([line_cos.T, -line_sin.T], axis=1),
            jnp.concatenate([line_sin.T, line_cos.T], axis=1),
        ],
        axis=0,
    )

    scale = points ** (-1.5)
    offset = lax.axis_index("grid") * depth
    def lanes_of(table):
        local = lax.dynamic_slice_in_dim(table.T.astype(jnp.float32) * scale, offset, depth, 1)
        return jnp.pad(jnp.tile(local, (1, conduction_bands)), ((0, 0), (0, LANES - used)))

    cos_lanes = lanes_of(line_cos)
    sin_lanes = lanes_of(line_sin)
    upper = (jnp.arange(parts) < bands)[None, :, None]
    cos_rows = jnp.broadcast_to(cos_lanes[:, None, :], (points, parts, LANES))
    sin_rows = jnp.broadcast_to(sin_lanes[:, None, :], (points, parts, LANES))
    cos_table = jnp.concatenate([cos_rows, jnp.where(upper, cos_rows, -cos_rows)], axis=0)
    sin_table = jnp.concatenate([jnp.where(upper, -sin_rows, sin_rows), -sin_rows], axis=0)

    line = grid_index // (points * points)
    remainder = grid_index % (points * points)
    row = remainder // points
    column = remainder % points
    mirrored = column >= half
    line = jnp.where(mirrored, points + (points - line) % points, line)
    row = jnp.where(mirrored, (points - row) % points, row)
    column = jnp.where(mirrored, points - column, column)
    place = (column * points + row) * (SUBLANES + 1)

    vmem = pl.BlockSpec(memory_space=pltpu.VMEM)
    smem = pl.BlockSpec(memory_space=pltpu.SMEM)
    return pl.pallas_call(
        functools.partial(spectra_kernel, points, half, half_pad, bands, 32),
        out_shape=jax.ShapeDtypeStruct(
            (grid_groups, valence_groups, columns, width), jnp.bfloat16
        ),
        in_specs=[smem, smem] + [vmem] * 8,
        out_specs=vmem,
        scratch_shapes=[
            pltpu.VMEM(
                ((parts * points // SUBLANES * half + SUBLANES) * (SUBLANES + 1), LANES), jnp.float32
            ),
            pltpu.VMEM((half * points * (SUBLANES + 1), LANES), jnp.float32),
            pltpu.VMEM((width * (SUBLANES + 1), LANES), jnp.float32),
        ],
        compiler_params=pltpu.CompilerParams(vmem_limit_bytes=60 * 2**20),
        name="spectra",
    )(
        place, line, valence, conduction, spread, z_table, y_table, cos_table, sin_table, fold,
    )


def exchange_kernel(
    part_ref, columns_ref, rows_ref, inbox, own, rs_send, rs_recv, row_send, row_recv, cond_send,
    cond_recv, grid_send, piece_recv, val_send, core_send,
):
    val_size, cond_size, grid_size = (lax.axis_size(name) for name in ("val", "cond", "grid"))
    val, cond, grid = (lax.axis_index(name) for name in ("val", "cond", "grid"))
    blocks = columns_ref.shape[3]
    group = val * cond_size + cond
    sibling = val + 1 - 2 * (val % 2)
    others = [(val + 2 * step) % val_size for step in range(1, val_size // 2)]
    grid_peers = [(grid + step) % grid_size for step in range(1, grid_size)]
    cond_peers = [(cond + step) % cond_size for step in range(1, cond_size)]
    group_size = val_size * cond_size
    group_peers = [(group + step) % group_size for step in range(1, group_size)]

    def copy(source, target, send, receive, device):
        return pltpu.make_async_remote_copy(
            src_ref=source, dst_ref=target, send_sem=send, recv_sem=receive, device_id=device,
            device_id_type=pl.DeviceIdType.MESH,
        )

    barrier = pltpu.get_barrier_semaphore()
    for peer in grid_peers:
        pl.semaphore_signal(
            barrier, inc=1, device_id=(val, cond, peer), device_id_type=pl.DeviceIdType.MESH
        )
    for peer in group_peers:
        pl.semaphore_signal(
            barrier, inc=1, device_id=(peer // cond_size, peer % cond_size, grid),
            device_id_type=pl.DeviceIdType.MESH,
        )
    pl.semaphore_wait(barrier, len(grid_peers) + len(group_peers))

    sent = []
    for step, peer in enumerate(grid_peers):
        sent.append(
            copy(
                part_ref.at[peer], inbox.at[step], rs_send.at[step], rs_recv.at[step],
                (val, cond, peer),
            )
        )
        sent[-1].start()
    for piece in sent:
        piece.wait_recv()
    for block in range(own.shape[0]):
        total = part_ref[grid, block].astype(jnp.float32)
        for step in range(grid_size - 1):
            total = total + inbox[step, block].astype(jnp.float32)
        own[block] = total.astype(own.dtype)

    cond_copies = []
    for step, peer in enumerate(cond_peers):
        cond_copies.append(
            copy(
                own.at[pl.ds(peer * blocks, blocks)], columns_ref.at[grid, val, cond],
                cond_send.at[step], cond_recv.at[step], (val, peer, grid),
            )
        )
        cond_copies[-1].start()
    columns_ref[grid, val, cond] = own[pl.ds(cond * blocks, blocks)]
    rows_ref[val, cond] = own[val]
    for piece in cond_copies:
        piece.wait_recv()
    sent += cond_copies

    def piece_copy(where, source_val, send, device):
        return copy(
            columns_ref.at[where, source_val], columns_ref.at[where, source_val], send,
            piece_recv.at[source_val * grid_size + where], device,
        )

    def spread(where, slot):
        for index, peer in enumerate(others):
            piece = piece_copy(
                where, val, val_send.at[index * grid_size + slot], (peer, cond, grid)
            )
            piece.start()
            sent.append(piece)
        forward(where, val, slot)

    def forward(where, source_val, slot):
        piece = piece_copy(where, source_val, core_send.at[slot], (sibling, cond, grid))
        piece.start()
        sent.append(piece)

    def arrive(where, source_val):
        piece_copy(where, source_val, core_send.at[0], (sibling, cond, grid)).wait_recv()

    for step, peer in enumerate(grid_peers):
        piece = piece_copy(grid, val, grid_send.at[step], (val, cond, peer))
        piece.start()
        sent.append(piece)
    spread(grid, 0)
    row_copies = []
    for step, peer in enumerate(group_peers):
        row_copies.append(
            copy(
                own.at[peer // cond_size], rows_ref.at[val, cond], row_send.at[step],
                row_recv.at[step], (peer // cond_size, peer % cond_size, grid),
            )
        )
        row_copies[-1].start()

    order = [0] + sorted(range(1, grid_size), key=lambda step: min(step, grid_size - step))
    places = [(grid + step) % grid_size for step in order]
    for slot in range(1, grid_size + 1):
        if slot < grid_size:
            arrive(places[slot], val)
            spread(places[slot], slot)
        for index, peer in enumerate(others):
            arrive(places[slot - 1], peer)
            forward(places[slot - 1], peer, grid_size * (index + 1) + slot - 1)
    for where in places:
        for source in [sibling] + [(sibling + 2 * step) % val_size for step in range(1, val_size // 2)]:
            arrive(where, source)
    for step, peer in enumerate(group_peers):
        source = (group + group_size - 1 - step) % group_size
        copy(
            own.at[0], rows_ref.at[source // cond_size, source % cond_size], row_send.at[step],
            row_recv.at[step], (peer // cond_size, peer % cond_size, grid),
        ).wait_recv()
    for piece in sent + row_copies:
        piece.wait_send()


def exchange(partial):
    val_size, cond_size, grid_size = (lax.axis_size(name) for name in ("val", "cond", "grid"))
    columns, width = partial.shape[2:]
    blocks = val_size // cond_size
    vmem = pl.BlockSpec(memory_space=pltpu.VMEM)
    kind = partial.dtype
    dma = pltpu.SemaphoreType.DMA
    return pl.pallas_call(
        exchange_kernel,
        out_shape=[
            jax.ShapeDtypeStruct((grid_size, val_size, cond_size, blocks, columns, width), kind),
            jax.ShapeDtypeStruct((val_size, cond_size, columns, width), kind),
        ],
        in_specs=[vmem],
        out_specs=[vmem, vmem],
        scratch_shapes=[
            pltpu.VMEM((grid_size - 1, val_size, columns, width), kind),
            pltpu.VMEM((val_size, columns, width), kind),
            dma((grid_size - 1,)),
            dma((grid_size - 1,)),
            dma((val_size * cond_size,)),
            dma((val_size * cond_size,)),
            dma((cond_size,)),
            dma((cond_size,)),
            dma((grid_size,)),
            dma((val_size * grid_size,)),
            dma((val_size * grid_size,)),
            dma((val_size * grid_size,)),
        ],
        compiler_params=pltpu.CompilerParams(
            collective_id=0, has_side_effects=True, vmem_limit_bytes=16 * 2**20
        ),
        name="exchange",
    )(partial)


def response_kernel(rows_ref, weights_ref, columns_ref, out_ref, left):
    depth = rows_ref.shape[0]
    width = rows_ref.shape[1]
    height = columns_ref.shape[-2]

    @pl.when((pl.program_id(0) == 0) & (pl.program_id(1) == 0))
    def scale_rows():
        scaled = rows_ref[...].astype(jnp.float32) * weights_ref[:, :1]
        pairs = scaled.reshape(-1, 2, height // 2, width)
        turned = jnp.concatenate([pairs[:, 1:], -pairs[:, :1]], axis=1).reshape(depth, width)
        left[:width] = scaled.T.astype(left.dtype)
        left[width:] = turned.T.astype(left.dtype)

    right = columns_ref[...].reshape(depth, columns_ref.shape[-1])
    out_ref[...] = jnp.dot(left[...], right, preferred_element_type=jnp.float32).reshape(
        out_ref.shape
    )


def response(rows, columns, weights):
    grid_size, val_size, cond_size, blocks, height, width = columns.shape
    depth = val_size * cond_size * height
    return pl.pallas_call(
        response_kernel,
        out_shape=jax.ShapeDtypeStruct((2, width, blocks * grid_size * width), jnp.float32),
        grid=(blocks, grid_size),
        in_specs=[
            pl.BlockSpec((depth, width), lambda block, place: (0, 0)),
            pl.BlockSpec((depth, LANES), lambda block, place: (0, 0)),
            pl.BlockSpec(
                (None, val_size, cond_size, None, height, width),
                lambda block, place: (place, 0, 0, block, 0, 0),
            ),
        ],
        out_specs=pl.BlockSpec(
            (2, width, width), lambda block, place: (0, 0, block * grid_size + place)
        ),
        scratch_shapes=[pltpu.VMEM((2 * width, depth), jnp.bfloat16)],
        compiler_params=pltpu.CompilerParams(vmem_limit_bytes=24 * 2**20),
        name="response",
    )(rows, weights, columns)


def local(valence_orbitals, conduction_orbitals, valence_energy, conduction_energy, grid_index):
    valence_groups = lax.axis_size("val")
    conduction_groups = lax.axis_size("cond")
    grid_groups = lax.axis_size("grid")
    valence_local = valence_orbitals.shape[0]
    conduction_local = conduction_orbitals.shape[0]
    pair_count = valence_local * conduction_local
    vectors = grid_index.shape[0]
    row_width = vectors // (valence_groups * grid_groups)
    column_width = vectors // conduction_groups
    groups = valence_groups * conduction_groups
    depth = groups * 2 * pair_count

    delta = valence_energy[:, None] - conduction_energy[None, :]
    all_pairs = valence_energy.shape[0] * conduction_energy.shape[0]
    weights = 4.0 * delta / (delta * delta + freq_squared) / math.sqrt(all_pairs)
    weights = weights.reshape(valence_groups, valence_local, conduction_groups, conduction_local)
    weights = jnp.transpose(weights, (0, 2, 1, 3)).reshape(groups, 1, pair_count, 1)

    partial = partial_spectra(valence_orbitals, conduction_orbitals, grid_index)
    if valence_groups % 2 == 0 and valence_groups % conduction_groups == 0 and grid_groups > 1:
        columns, rows = exchange(partial)
        spread = jnp.broadcast_to(weights, (groups, 2, pair_count, LANES)).reshape(depth, LANES)
        return response(rows.reshape(depth, row_width), columns, spread)

    arrived = lax.all_to_all(partial, "grid", split_axis=0, concat_axis=0, tiled=True)
    own = jnp.sum(arrived.astype(jnp.float32), axis=0).astype(jnp.bfloat16)
    everything = lax.all_gather(own, ("val", "cond"), axis=0, tiled=False)
    rows = lax.dynamic_index_in_dim(everything, lax.axis_index("val"), 1, keepdims=False)
    rows = rows.reshape(groups, 2, pair_count, row_width)
    columns = lax.all_gather(jnp.swapaxes(everything, 1, 2), "grid", axis=3, tiled=False)
    columns = lax.dynamic_slice_in_dim(
        columns.reshape(depth, vectors), lax.axis_index("cond") * column_width, column_width, 1
    )
    scaled = (rows.astype(jnp.float32) * weights).astype(jnp.bfloat16)
    turned = jnp.stack([scaled[:, 1], -scaled[:, 0]], axis=1)
    both = jnp.stack([scaled, turned], axis=0).reshape(2, depth, row_width)
    return lax.dot_general(
        both, columns, (((1,), (0,)), ((), ())), preferred_element_type=jnp.float32
    )


def solution(mesh):
    return jax.shard_map(
        local,
        mesh=mesh,
        in_specs=(P("val", "grid", None), P("cond", "grid", None), P(), P(), P()),
        out_specs=P(None, ("val", "grid"), "cond"),
        check_vma=False,
    )
```

```python
import functools
import math

import jax
import jax.numpy as jnp
import numpy as np
from jax import lax
from jax.experimental import pallas as pl
from jax.experimental.pallas import tpu as pltpu
from jax.sharding import PartitionSpec as P

freq_squared = 4.0
LANES = 128
SUBLANES = 8
INPUTS = 10


def line_tables(points):
    indices = jnp.arange(points, dtype=jnp.int32)
    phases = indices[:, None] * indices[None, :] % points
    angles = phases.astype(jnp.float32) * (2.0 * math.pi / points)
    return (jnp.cos(angles).astype(jnp.bfloat16), (-jnp.sin(angles)).astype(jnp.bfloat16))


def spectra_steps(
    points, half, half_pad, bands, unroll, width,
    row_ref, line_ref, valence_ref, conduction_ref, spread_ref, z_ref, y_ref, cos_ref, sin_ref,
    fold_ref, lines, planes, picked,
):
    parts = 2 * bands
    groups = points // SUBLANES
    pitch = SUBLANES + 1
    depth = valence_ref.shape[1]
    used = conduction_ref.shape[0] * depth

    def z_pass(group):
        span = SUBLANES * points
        place = pl.ds(pl.multiple_of(group * span, LANES), span)
        valence = valence_ref[:, :, place].astype(jnp.float32).reshape(bands * depth, span)
        conduction = conduction_ref[:, :, place].astype(jnp.float32).reshape(used, span)
        if used < LANES:
            conduction = jnp.concatenate(
                [conduction, jnp.zeros((LANES - used, span), jnp.float32)], axis=0
            )
        wide = jnp.dot(
            valence.T.astype(jnp.bfloat16), spread_ref[...], preferred_element_type=jnp.float32
        )
        products = (wide * jnp.concatenate([conduction.T] * bands, axis=1)).astype(jnp.bfloat16)
        for inner in range(SUBLANES):
            result = jnp.dot(
                z_ref[...],
                products[inner * points : (inner + 1) * points],
                preferred_element_type=jnp.float32,
            )
            for part in range(parts):
                kind, band = part // bands, part % bands
                start = (part * groups + group) * half * pitch + inner
                lines[pl.ds(start, half, stride=pitch), :] = result[
                    kind * half_pad : kind * half_pad + half, band * LANES : (band + 1) * LANES
                ]

    def y_pass(q):
        def slab(part):
            return jnp.concatenate(
                [
                    lines[pl.ds(((part * groups + group) * half + q) * pitch, SUBLANES), :]
                    for group in range(groups)
                ],
                axis=0,
            )

        block = jnp.concatenate(
            [
                jnp.concatenate([slab(kind * bands + band) for band in range(bands)], axis=1)
                for kind in range(2)
            ],
            axis=0,
        ).astype(jnp.bfloat16)
        result = jnp.dot(y_ref[...], block, preferred_element_type=jnp.float32)
        for part in range(parts):
            kind, band = part // bands, part % bands
            planes[pl.ds(q * points * pitch + part, points, stride=pitch), :] = result[
                kind * points : (kind + 1) * points, band * LANES : (band + 1) * LANES
            ]

    def pick(place, block, out_ref):
        first = (block * out_ref.shape[0] + place) * width

        def some(step, carry):
            found = []
            for inner in range(unroll):
                vector = first + step * unroll + inner
                line = line_ref[vector]
                values = planes[pl.ds(row_ref[vector], parts), :]
                swapped = pltpu.roll(values, bands, axis=0)
                found.append(values * cos_ref[line] + swapped * sin_ref[line])
            for inner in range(unroll):
                picked[pl.ds((step * unroll + inner) * pitch, parts), :] = found[inner]
            return carry

        lax.fori_loop(0, width // unroll, some, 0)
        rows = jnp.concatenate(
            [picked[pl.ds(part, width, stride=pitch), :].astype(jnp.bfloat16) for part in range(parts)],
            axis=1,
        )
        folded = jnp.dot(rows, fold_ref[...], preferred_element_type=jnp.float32)
        out_ref[place, block] = folded.T[: out_ref.shape[2], :].astype(out_ref.dtype)

    def loop(count, body, step):
        def several(index, carry):
            for inner in range(step):
                body(index * step + inner)
            return carry

        lax.fori_loop(0, count // step, several, 0)
        for rest in range(count - count % step, count):
            body(rest)

    def transform():
        loop(groups, z_pass, 1)
        loop(half, y_pass, 4)

    return transform, pick


def spectra_kernel(sizes, *refs):
    out_ref = refs[INPUTS]
    transform, pick = spectra_steps(*sizes, *refs[:INPUTS], *refs[INPUTS + 1 :])
    transform()

    def tile(index, carry):
        pick(index % out_ref.shape[0], index // out_ref.shape[0], out_ref)
        return carry

    lax.fori_loop(0, out_ref.shape[0] * out_ref.shape[1], tile, 0)


def partial_spectra(valence, conduction, grid_index, remote):
    valence_groups = lax.axis_size("val")
    grid_groups = lax.axis_size("grid")
    bands, depth, plane = valence.shape
    conduction_bands = conduction.shape[0]
    points = depth * lax.axis_size("grid")
    half = points // 2 + 1
    half_pad = -(-half // 16) * 16
    used = conduction_bands * depth
    parts = 2 * bands
    vectors = grid_index.shape[0]
    width = vectors // (grid_groups * valence_groups)
    line_cos, line_sin = line_tables(points)

    spread = np.zeros((bands * depth, bands, LANES), np.float32)
    for band in range(bands):
        for other in range(conduction_bands):
            for x in range(depth):
                spread[band * depth + x, band, other * depth + x] = 1.0
    spread = jnp.asarray(spread.reshape(bands * depth, bands * LANES), jnp.bfloat16)
    columns = parts * conduction_bands
    fold = np.zeros((parts, LANES, LANES), np.float32)
    for part in range(parts):
        for other in range(conduction_bands):
            fold[part, other * depth : (other + 1) * depth, part * conduction_bands + other] = 1.0
    fold = jnp.asarray(fold.reshape(parts * LANES, LANES), jnp.bfloat16)

    z_table = jnp.zeros((2 * half_pad, points), jnp.bfloat16)
    z_table = z_table.at[:half].set(line_cos.T[:half])
    z_table = z_table.at[half_pad : half_pad + half].set(line_sin.T[:half])
    y_table = jnp.concatenate(
        [
            jnp.concatenate([line_cos.T, -line_sin.T], axis=1),
            jnp.concatenate([line_sin.T, line_cos.T], axis=1),
        ],
        axis=0,
    )

    scale = points ** (-1.5)
    offset = lax.axis_index("grid") * depth
    def lanes_of(table):
        local = lax.dynamic_slice_in_dim(table.T.astype(jnp.float32) * scale, offset, depth, 1)
        return jnp.pad(jnp.tile(local, (1, conduction_bands)), ((0, 0), (0, LANES - used)))

    cos_lanes = lanes_of(line_cos)
    sin_lanes = lanes_of(line_sin)
    upper = (jnp.arange(parts) < bands)[None, :, None]
    cos_rows = jnp.broadcast_to(cos_lanes[:, None, :], (points, parts, LANES))
    sin_rows = jnp.broadcast_to(sin_lanes[:, None, :], (points, parts, LANES))
    cos_table = jnp.concatenate([cos_rows, jnp.where(upper, cos_rows, -cos_rows)], axis=0)
    sin_table = jnp.concatenate([jnp.where(upper, -sin_rows, sin_rows), -sin_rows], axis=0)

    line = grid_index // (points * points)
    remainder = grid_index % (points * points)
    row = remainder // points
    column = remainder % points
    mirrored = column >= half
    line = jnp.where(mirrored, points + (points - line) % points, line)
    row = jnp.where(mirrored, (points - row) % points, row)
    column = jnp.where(mirrored, points - column, column)
    place = (column * points + row) * (SUBLANES + 1)

    operands = (
        place, line, valence, conduction, spread, z_table, y_table, cos_table, sin_table, fold,
    )
    sizes = (points, half, half_pad, bands, 32, width)
    scratch = [
        pltpu.VMEM(
            ((parts * points // SUBLANES * half + SUBLANES) * (SUBLANES + 1), LANES), jnp.float32
        ),
        pltpu.VMEM((half * points * (SUBLANES + 1), LANES), jnp.float32),
        pltpu.VMEM((width * (SUBLANES + 1), LANES), jnp.float32),
    ]
    partial = (grid_groups, valence_groups, columns, width)
    vmem = pl.BlockSpec(memory_space=pltpu.VMEM)
    smem = pl.BlockSpec(memory_space=pltpu.SMEM)
    specs = [smem, smem] + [vmem] * (INPUTS - 2)
    if not remote:
        return pl.pallas_call(
            functools.partial(spectra_kernel, sizes),
            out_shape=jax.ShapeDtypeStruct(partial, jnp.bfloat16),
            in_specs=specs,
            out_specs=vmem,
            scratch_shapes=scratch,
            compiler_params=pltpu.CompilerParams(vmem_limit_bytes=60 * 2**20),
            name="spectra",
        )(*operands)
    cond_groups = lax.axis_size("cond")
    blocks = valence_groups // cond_groups
    groups = valence_groups * cond_groups
    dma = pltpu.SemaphoreType.DMA
    return pl.pallas_call(
        functools.partial(exchange_kernel, sizes),
        out_shape=[
            jax.ShapeDtypeStruct(
                (grid_groups, blocks, valence_groups, cond_groups, columns, width), jnp.bfloat16
            ),
            jax.ShapeDtypeStruct((valence_groups, cond_groups, columns, width), jnp.bfloat16),
        ],
        in_specs=specs,
        out_specs=[vmem, vmem],
        scratch_shapes=scratch
        + [
            pltpu.VMEM(partial, jnp.bfloat16),
            pltpu.VMEM((grid_groups - 1,) + partial[1:], jnp.bfloat16),
            pltpu.VMEM(partial[1:], jnp.bfloat16),
            dma(((grid_groups - 1) * valence_groups,)),
            dma(((grid_groups - 1) * valence_groups,)),
            dma((groups,)),
            dma((groups,)),
            dma((blocks * cond_groups,)),
            dma((blocks * cond_groups,)),
            dma((blocks * grid_groups,)),
            dma((blocks * valence_groups * grid_groups,)),
            dma((blocks * valence_groups * grid_groups,)),
            dma((blocks * valence_groups * grid_groups,)),
        ],
        compiler_params=pltpu.CompilerParams(
            collective_id=0, has_side_effects=True, vmem_limit_bytes=60 * 2**20
        ),
        name="spectra_exchange",
    )(*operands)


def exchange_kernel(sizes, *refs):
    columns_ref, rows_ref = refs[INPUTS : INPUTS + 2]
    lines, planes, picked, part_ref, inbox, own = refs[INPUTS + 2 : INPUTS + 8]
    (
        rs_send, rs_recv, row_send, row_recv, cond_send, cond_recv, grid_send, piece_recv, val_send,
        core_send,
    ) = refs[INPUTS + 8 :]
    transform, pick = spectra_steps(*sizes, *refs[:INPUTS], lines, planes, picked)
    val_size, cond_size, grid_size = (lax.axis_size(name) for name in ("val", "cond", "grid"))
    val, cond, grid = (lax.axis_index(name) for name in ("val", "cond", "grid"))
    blocks = val_size // cond_size
    group = val * cond_size + cond
    sibling = val + 1 - 2 * (val % 2)
    others = [(val + 2 * step) % val_size for step in range(1, val_size // 2)]
    across = [(sibling + 2 * step) % val_size for step in range(val_size // 2)]
    grid_peers = [(grid + step) % grid_size for step in range(1, grid_size)]
    cond_peers = [(cond + step) % cond_size for step in range(1, cond_size)]
    group_size = val_size * cond_size
    group_peers = [(group + step) % group_size for step in range(1, group_size)]
    order = [0] + sorted(range(1, grid_size), key=lambda step: min(step, grid_size - step))
    places = [(grid + step) % grid_size for step in order]

    def copy(source, target, send, receive, device):
        return pltpu.make_async_remote_copy(
            src_ref=source, dst_ref=target, send_sem=send, recv_sem=receive, device_id=device,
            device_id_type=pl.DeviceIdType.MESH,
        )

    barrier = pltpu.get_barrier_semaphore()
    for peer in grid_peers:
        pl.semaphore_signal(
            barrier, inc=1, device_id=(val, cond, peer), device_id_type=pl.DeviceIdType.MESH
        )
    for peer in group_peers:
        pl.semaphore_signal(
            barrier, inc=1, device_id=(peer // cond_size, peer % cond_size, grid),
            device_id_type=pl.DeviceIdType.MESH,
        )
    transform()
    pl.semaphore_wait(barrier, len(grid_peers) + len(group_peers))

    def partial_copy(step, block):
        peer = (grid + step) % grid_size
        slot = (step - 1) * val_size + block
        return copy(
            part_ref.at[peer, block], inbox.at[step - 1, block], rs_send.at[slot],
            rs_recv.at[slot], (val, cond, peer),
        )

    def pick_remote(turn, first, last):
        def one(index, carry):
            step = index // cond_size + 1
            block = index % cond_size * blocks + turn
            pick((grid + step) % grid_size, block, part_ref)
            partial_copy(step, block).start()
            return carry

        lax.fori_loop(first, last, one, 0)

    def pick_own(turn):
        def one(index, carry):
            pick(grid, index * blocks + turn, part_ref)
            return carry

        lax.fori_loop(0, cond_size, one, 0)

    def cond_copy(turn, step):
        peer = (cond + step) % cond_size
        return copy(
            own.at[peer * blocks + turn], columns_ref.at[grid, turn, val, cond],
            cond_send.at[turn * cond_size + step], cond_recv.at[turn * cond_size + step],
            (val, peer, grid),
        )

    def row_copy(step, source):
        peer = (group + step) % group_size
        return copy(
            own.at[peer // cond_size], rows_ref.at[source // cond_size, source % cond_size],
            row_send.at[step], row_recv.at[step], (peer // cond_size, peer % cond_size, grid),
        )

    def reduce_own(turn):
        for part in range(cond_size):
            block = part * blocks + turn
            total = part_ref[grid, block].astype(jnp.float32)
            for step in range(1, grid_size):
                partial_copy(step, block).wait_recv()
                total = total + inbox[step - 1, block].astype(jnp.float32)
            own[block] = total.astype(own.dtype)
        for step in range(1, cond_size):
            cond_copy(turn, step).start()
        columns_ref[grid, turn, val, cond] = own[cond * blocks + turn]

    def send_rows(turn):
        for step in range(1, group_size):

            @pl.when((group + step) % group_size // cond_size % blocks == turn)
            def start():
                row_copy(step, group).start()

    sent = []

    def piece_copy(turn, where, source_val, send, device):
        piece = columns_ref.at[where, turn, source_val]
        receive = piece_recv.at[(turn * val_size + source_val) * grid_size + where]
        return copy(piece, piece, send, receive, device)

    def start(piece):
        piece.start()
        sent.append(piece)

    def forward(turn, where, source_val, slot):
        send = core_send.at[turn * val_size * grid_size + slot]
        start(piece_copy(turn, where, source_val, send, (sibling, cond, grid)))

    def spread(turn, where, slot):
        for index, peer in enumerate(others):
            send = val_send.at[(turn * val_size + index) * grid_size + slot]
            start(piece_copy(turn, where, val, send, (peer, cond, grid)))
        forward(turn, where, val, slot)

    def arrive(turn, where, source_val):
        piece_copy(turn, where, source_val, core_send.at[0], (sibling, cond, grid)).wait_recv()

    def send_own(turn):
        for step in range(1, cond_size):
            cond_copy(turn, step).wait_recv()
        for step, peer in enumerate(grid_peers):
            send = grid_send.at[turn * grid_size + step]
            start(piece_copy(turn, grid, val, send, (val, cond, peer)))
        spread(turn, grid, 0)

    def pass_on(turn):
        for slot in range(1, grid_size + 1):
            if slot < grid_size:
                arrive(turn, places[slot], val)
                spread(turn, places[slot], slot)
            for index, peer in enumerate(others):
                arrive(turn, places[slot - 1], peer)
                forward(turn, places[slot - 1], peer, grid_size * (index + 1) + slot - 1)

    tiles = cond_size * (grid_size - 1)
    for turn in range(blocks):
        if turn == 0:
            pick_remote(turn, 0, tiles)
        else:
            pick_remote(turn, 0, tiles // 3)
            reduce_own(turn - 1)
            send_rows(turn - 1)
            pick_remote(turn, tiles // 3, tiles * 2 // 3)
            send_own(turn - 1)
            pick_remote(turn, tiles * 2 // 3, tiles)
        pick_own(turn)
        if turn >= 2:
            pass_on(turn - 2)
    reduce_own(blocks - 1)
    send_rows(blocks - 1)
    rows_ref[val, cond] = own[val]
    send_own(blocks - 1)
    for turn in range(max(blocks - 2, 0), blocks):
        pass_on(turn)
    for turn in range(blocks):
        for where in places:
            for source in across:
                arrive(turn, where, source)
    for step in range(1, group_size):
        row_copy(step, (group + group_size - step) % group_size).wait_recv()
        row_copy(step, group).wait_send()
    for turn in range(blocks):
        for step in range(1, cond_size):
            cond_copy(turn, step).wait_send()
    for step in range(1, grid_size):
        for block in range(val_size):
            partial_copy(step, block).wait_send()
    for piece in sent:
        piece.wait_send()


def response_kernel(rows_ref, weights_ref, columns_ref, out_ref, left):
    depth = rows_ref.shape[0]
    width = rows_ref.shape[1]
    height = columns_ref.shape[-2]

    @pl.when((pl.program_id(0) == 0) & (pl.program_id(1) == 0))
    def scale_rows():
        scaled = rows_ref[...].astype(jnp.float32) * weights_ref[:, :1]
        pairs = scaled.reshape(-1, 2, height // 2, width)
        turned = jnp.concatenate([pairs[:, 1:], -pairs[:, :1]], axis=1).reshape(depth, width)
        left[:width] = scaled.T.astype(left.dtype)
        left[width:] = turned.T.astype(left.dtype)

    right = columns_ref[...].reshape(depth, columns_ref.shape[-1])
    out_ref[...] = jnp.dot(left[...], right, preferred_element_type=jnp.float32).reshape(
        out_ref.shape
    )


def response(rows, columns, weights):
    grid_size, blocks, val_size, cond_size, height, width = columns.shape
    depth = val_size * cond_size * height
    return pl.pallas_call(
        response_kernel,
        out_shape=jax.ShapeDtypeStruct((2, width, blocks * grid_size * width), jnp.float32),
        grid=(blocks, grid_size),
        in_specs=[
            pl.BlockSpec((depth, width), lambda block, place: (0, 0)),
            pl.BlockSpec((depth, LANES), lambda block, place: (0, 0)),
            pl.BlockSpec(
                (None, None, val_size, cond_size, height, width),
                lambda block, place: (place, block, 0, 0, 0, 0),
            ),
        ],
        out_specs=pl.BlockSpec(
            (2, width, width), lambda block, place: (0, 0, block * grid_size + place)
        ),
        scratch_shapes=[pltpu.VMEM((2 * width, depth), jnp.bfloat16)],
        compiler_params=pltpu.CompilerParams(vmem_limit_bytes=24 * 2**20),
        name="response",
    )(rows, weights, columns)


def local(valence_orbitals, conduction_orbitals, valence_energy, conduction_energy, grid_index):
    valence_groups = lax.axis_size("val")
    conduction_groups = lax.axis_size("cond")
    grid_groups = lax.axis_size("grid")
    valence_local = valence_orbitals.shape[0]
    conduction_local = conduction_orbitals.shape[0]
    pair_count = valence_local * conduction_local
    vectors = grid_index.shape[0]
    row_width = vectors // (valence_groups * grid_groups)
    column_width = vectors // conduction_groups
    groups = valence_groups * conduction_groups
    depth = groups * 2 * pair_count

    delta = valence_energy[:, None] - conduction_energy[None, :]
    all_pairs = valence_energy.shape[0] * conduction_energy.shape[0]
    weights = 4.0 * delta / (delta * delta + freq_squared) / math.sqrt(all_pairs)
    weights = weights.reshape(valence_groups, valence_local, conduction_groups, conduction_local)
    weights = jnp.transpose(weights, (0, 2, 1, 3)).reshape(groups, 1, pair_count, 1)

    remote = valence_groups % 2 == 0 and valence_groups % conduction_groups == 0
    remote = remote and grid_groups > 1
    result = partial_spectra(valence_orbitals, conduction_orbitals, grid_index, remote)
    if remote:
        columns, rows = result
        spread = jnp.broadcast_to(weights, (groups, 2, pair_count, LANES)).reshape(depth, LANES)
        return response(rows.reshape(depth, row_width), columns, spread)

    arrived = lax.all_to_all(result, "grid", split_axis=0, concat_axis=0, tiled=True)
    own = jnp.sum(arrived.astype(jnp.float32), axis=0).astype(jnp.bfloat16)
    everything = lax.all_gather(own, ("val", "cond"), axis=0, tiled=False)
    rows = lax.dynamic_index_in_dim(everything, lax.axis_index("val"), 1, keepdims=False)
    rows = rows.reshape(groups, 2, pair_count, row_width)
    columns = lax.all_gather(jnp.swapaxes(everything, 1, 2), "grid", axis=3, tiled=False)
    columns = lax.dynamic_slice_in_dim(
        columns.reshape(depth, vectors), lax.axis_index("cond") * column_width, column_width, 1
    )
    scaled = (rows.astype(jnp.float32) * weights).astype(jnp.bfloat16)
    turned = jnp.stack([scaled[:, 1], -scaled[:, 0]], axis=1)
    both = jnp.stack([scaled, turned], axis=0).reshape(2, depth, row_width)
    return lax.dot_general(
        both, columns, (((1,), (0,)), ((), ())), preferred_element_type=jnp.float32
    )


def solution(mesh):
    return jax.shard_map(
        local,
        mesh=mesh,
        in_specs=(P("val", "grid", None), P("cond", "grid", None), P(), P(), P()),
        out_specs=P(None, ("val", "grid"), "cond"),
        check_vma=False,
    )
```

```python
import functools
import math

import jax
import jax.numpy as jnp
import ml_dtypes
import numpy as np
from jax import lax
from jax.experimental import pallas as pl
from jax.experimental.pallas import tpu as pltpu
from jax.sharding import PartitionSpec as P

freq_squared = 4.0
LANES = 128
SUBLANES = 8
INPUTS = 9


def line_tables(points):
    indices = np.arange(points, dtype=np.int32)
    phases = indices[:, None] * indices[None, :] % points
    angles = phases.astype(np.float32) * np.float32(2.0 * math.pi / points)
    return (np.cos(angles).astype(ml_dtypes.bfloat16), (-np.sin(angles)).astype(ml_dtypes.bfloat16))


def spectra_steps(
    points, half, half_pad, bands, unroll, width,
    index_ref, valence_ref, conduction_ref, spread_ref, z_ref, y_ref, x_cos_ref, x_sin_ref,
    fold_ref, lines, planes, picked, cos_ref, sin_ref,
):
    parts = 2 * bands
    groups = points // SUBLANES
    pitch = SUBLANES + 1
    depth = valence_ref.shape[1]
    used = conduction_ref.shape[0] * depth
    line_bits = (2 * points - 1).bit_length()

    def fill(group):
        rows = pl.ds(pl.multiple_of(group * SUBLANES, SUBLANES), SUBLANES)
        cos_block = x_cos_ref[lax.axis_index("grid"), rows, :]
        sin_block = x_sin_ref[lax.axis_index("grid"), rows, :]
        upper = lax.broadcasted_iota(jnp.int32, (parts, LANES), 0) < bands
        for inner in range(SUBLANES):
            cos_row = jnp.broadcast_to(cos_block[inner : inner + 1], (parts, LANES))
            sin_row = jnp.broadcast_to(sin_block[inner : inner + 1], (parts, LANES))
            line = group * SUBLANES + inner
            cos_ref[line] = cos_row
            sin_ref[line] = jnp.where(upper, -sin_row, sin_row)
            cos_ref[points + line] = jnp.where(upper, cos_row, -cos_row)
            sin_ref[points + line] = -sin_row

    def z_pass(group):
        span = SUBLANES * points
        place = pl.ds(pl.multiple_of(group * span, LANES), span)
        valence = valence_ref[:, :, place].astype(jnp.float32).reshape(bands * depth, span)
        conduction = conduction_ref[:, :, place].astype(jnp.float32).reshape(used, span)
        if used < LANES:
            conduction = jnp.concatenate(
                [conduction, jnp.zeros((LANES - used, span), jnp.float32)], axis=0
            )
        wide = jnp.dot(
            valence.T.astype(jnp.bfloat16), spread_ref[...], preferred_element_type=jnp.float32
        )
        products = (wide * jnp.concatenate([conduction.T] * bands, axis=1)).astype(jnp.bfloat16)
        for inner in range(SUBLANES):
            result = jnp.dot(
                z_ref[...],
                products[inner * points : (inner + 1) * points],
                preferred_element_type=jnp.float32,
            )
            for part in range(parts):
                kind, band = part // bands, part % bands
                start = (part * groups + group) * half * pitch + inner
                lines[pl.ds(start, half, stride=pitch), :] = result[
                    kind * half_pad : kind * half_pad + half, band * LANES : (band + 1) * LANES
                ]

    def y_pass(q):
        def slab(part):
            return jnp.concatenate(
                [
                    lines[pl.ds(((part * groups + group) * half + q) * pitch, SUBLANES), :]
                    for group in range(groups)
                ],
                axis=0,
            )

        block = jnp.concatenate(
            [
                jnp.concatenate([slab(kind * bands + band) for band in range(bands)], axis=1)
                for kind in range(2)
            ],
            axis=0,
        ).astype(jnp.bfloat16)
        result = jnp.dot(y_ref[...], block, preferred_element_type=jnp.float32)
        for part in range(parts):
            kind, band = part // bands, part % bands
            planes[pl.ds(q * points * pitch + part, points, stride=pitch), :] = result[
                kind * points : (kind + 1) * points, band * LANES : (band + 1) * LANES
            ]

    def pick(place, block, out_ref):
        first = (block * out_ref.shape[0] + place) * width

        def some(step, carry):
            found = []
            for inner in range(unroll):
                vector = first + step * unroll + inner
                word = index_ref[vector]
                line = lax.bitwise_and(word, 2**line_bits - 1)
                row = lax.shift_right_logical(word, line_bits)
                values = planes[pl.ds(row, parts), :]
                swapped = pltpu.roll(values, bands, axis=0)
                found.append(values * cos_ref[line] + swapped * sin_ref[line])
            for inner in range(unroll):
                picked[pl.ds((step * unroll + inner) * pitch, parts), :] = found[inner]
            return carry

        lax.fori_loop(0, width // unroll, some, 0)
        rows = jnp.concatenate(
            [picked[pl.ds(part, width, stride=pitch), :].astype(jnp.bfloat16) for part in range(parts)],
            axis=1,
        )
        folded = jnp.dot(rows, fold_ref[...], preferred_element_type=jnp.float32)
        out_ref[place, block] = folded.T[: out_ref.shape[2], :].astype(out_ref.dtype)

    def loop(count, body, step):
        def several(index, carry):
            for inner in range(step):
                body(index * step + inner)
            return carry

        lax.fori_loop(0, count // step, several, 0)
        for rest in range(count - count % step, count):
            body(rest)

    def transform():
        loop(groups, fill, 1)
        loop(groups, z_pass, 1)
        loop(half, y_pass, 4)

    return transform, pick


def spectra_kernel(sizes, *refs):
    out_ref = refs[INPUTS]
    transform, pick = spectra_steps(*sizes, *refs[:INPUTS], *refs[INPUTS + 1 :])
    transform()

    def tile(index, carry):
        pick(index % out_ref.shape[0], index // out_ref.shape[0], out_ref)
        return carry

    lax.fori_loop(0, out_ref.shape[0] * out_ref.shape[1], tile, 0)


def partial_spectra(valence, conduction, grid_index, remote):
    valence_groups = lax.axis_size("val")
    grid_groups = lax.axis_size("grid")
    bands, depth, plane = valence.shape
    conduction_bands = conduction.shape[0]
    points = depth * lax.axis_size("grid")
    half = points // 2 + 1
    half_pad = -(-half // 16) * 16
    used = conduction_bands * depth
    parts = 2 * bands
    vectors = grid_index.shape[0]
    width = vectors // (grid_groups * valence_groups)
    line_cos, line_sin = line_tables(points)

    spread = np.zeros((bands * depth, bands, LANES), np.float32)
    for band in range(bands):
        for other in range(conduction_bands):
            for x in range(depth):
                spread[band * depth + x, band, other * depth + x] = 1.0
    spread = spread.reshape(bands * depth, bands * LANES).astype(ml_dtypes.bfloat16)
    columns = parts * conduction_bands
    fold = np.zeros((parts, LANES, LANES), np.float32)
    for part in range(parts):
        for other in range(conduction_bands):
            fold[part, other * depth : (other + 1) * depth, part * conduction_bands + other] = 1.0
    fold = fold.reshape(parts * LANES, LANES).astype(ml_dtypes.bfloat16)

    z_table = np.zeros((2 * half_pad, points), ml_dtypes.bfloat16)
    z_table[:half] = line_cos.T[:half]
    z_table[half_pad : half_pad + half] = line_sin.T[:half]
    y_table = np.concatenate(
        [
            np.concatenate([line_cos.T, -line_sin.T], axis=1),
            np.concatenate([line_sin.T, line_cos.T], axis=1),
        ],
        axis=0,
    )

    def lanes_of(table):
        lanes = np.zeros((grid_groups, points, LANES), np.float32)
        for place in range(grid_groups):
            own = table[place * depth : (place + 1) * depth].T.astype(np.float32)
            lanes[place, :, :used] = np.tile(own * np.float32(points ** (-1.5)), (1, conduction_bands))
        return lanes

    line = grid_index // (points * points)
    remainder = grid_index % (points * points)
    row = remainder // points
    column = remainder % points
    mirrored = column >= half
    line = jnp.where(mirrored, points + (points - line) % points, line)
    row = jnp.where(mirrored, (points - row) % points, row)
    column = jnp.where(mirrored, points - column, column)
    place = (column * points + row) * (SUBLANES + 1)
    index = place * 2 ** (2 * points - 1).bit_length() + line

    operands = (
        index, valence, conduction, spread, z_table, y_table, lanes_of(line_cos),
        lanes_of(line_sin), fold,
    )
    sizes = (points, half, half_pad, bands, 32, width)
    scratch = [
        pltpu.VMEM(
            ((parts * points // SUBLANES * half + SUBLANES) * (SUBLANES + 1), LANES), jnp.float32
        ),
        pltpu.VMEM((half * points * (SUBLANES + 1), LANES), jnp.float32),
        pltpu.VMEM((width * (SUBLANES + 1), LANES), jnp.float32),
        pltpu.VMEM((2 * points, parts, LANES), jnp.float32),
        pltpu.VMEM((2 * points, parts, LANES), jnp.float32),
    ]
    partial = (grid_groups, valence_groups, columns, width)
    vmem = pl.BlockSpec(memory_space=pltpu.VMEM)
    smem = pl.BlockSpec(memory_space=pltpu.SMEM)
    specs = [smem] + [vmem] * (INPUTS - 1)
    if not remote:
        return pl.pallas_call(
            functools.partial(spectra_kernel, sizes),
            out_shape=jax.ShapeDtypeStruct(partial, jnp.bfloat16),
            in_specs=specs,
            out_specs=vmem,
            scratch_shapes=scratch,
            compiler_params=pltpu.CompilerParams(vmem_limit_bytes=60 * 2**20),
            name="spectra",
        )(*operands)
    cond_groups = lax.axis_size("cond")
    blocks = valence_groups // cond_groups
    groups = valence_groups * cond_groups
    dma = pltpu.SemaphoreType.DMA
    return pl.pallas_call(
        functools.partial(exchange_kernel, sizes),
        out_shape=[
            jax.ShapeDtypeStruct(
                (grid_groups, blocks, valence_groups, cond_groups, columns, width), jnp.bfloat16
            ),
            jax.ShapeDtypeStruct((valence_groups, cond_groups, columns, width), jnp.bfloat16),
        ],
        in_specs=specs,
        out_specs=[vmem, vmem],
        scratch_shapes=scratch
        + [
            pltpu.VMEM(partial, jnp.bfloat16),
            pltpu.VMEM((grid_groups - 1,) + partial[1:], jnp.bfloat16),
            pltpu.VMEM(partial[1:], jnp.bfloat16),
            dma(((grid_groups - 1) * valence_groups,)),
            dma(((grid_groups - 1) * valence_groups,)),
            dma((groups,)),
            dma((groups,)),
            dma((blocks * cond_groups * grid_groups,)),
            dma((blocks * cond_groups * grid_groups,)),
            dma((blocks * valence_groups * grid_groups,)),
            dma((blocks * valence_groups * grid_groups,)),
            dma((blocks * valence_groups * grid_groups,)),
        ],
        compiler_params=pltpu.CompilerParams(
            collective_id=0, has_side_effects=True, vmem_limit_bytes=60 * 2**20
        ),
        name="spectra_exchange",
    )(*operands)


def exchange_kernel(sizes, *refs):
    columns_ref, rows_ref = refs[INPUTS : INPUTS + 2]
    part_ref, inbox, own = refs[INPUTS + 7 : INPUTS + 10]
    (
        rs_send, rs_recv, row_send, row_recv, own_send, own_recv, piece_recv, val_send, core_send,
    ) = refs[INPUTS + 10 :]
    transform, pick = spectra_steps(*sizes, *refs[:INPUTS], *refs[INPUTS + 2 : INPUTS + 7])
    val_size, cond_size, grid_size = (lax.axis_size(name) for name in ("val", "cond", "grid"))
    val, cond, grid = (lax.axis_index(name) for name in ("val", "cond", "grid"))
    blocks = val_size // cond_size
    group = val * cond_size + cond
    sibling = val + 1 - 2 * (val % 2)
    others = [(val + 2 * step) % val_size for step in range(1, val_size // 2)]
    across = [(sibling + 2 * step) % val_size for step in range(val_size // 2)]
    grid_peers = [(grid + step) % grid_size for step in range(1, grid_size)]
    group_size = val_size * cond_size
    group_peers = [(group + step) % group_size for step in range(1, group_size)]
    order = [0] + sorted(range(1, grid_size), key=lambda step: min(step, grid_size - step))
    places = [(grid + step) % grid_size for step in order]

    def copy(source, target, send, receive, device):
        return pltpu.make_async_remote_copy(
            src_ref=source, dst_ref=target, send_sem=send, recv_sem=receive, device_id=device,
            device_id_type=pl.DeviceIdType.MESH,
        )

    barrier = pltpu.get_barrier_semaphore()
    line_peers = [
        ((cond + step) % cond_size, peer) for step in range(cond_size) for peer in grid_peers
    ]
    for peer in line_peers:
        pl.semaphore_signal(
            barrier, inc=1, device_id=(val, *peer), device_id_type=pl.DeviceIdType.MESH
        )
    for peer in group_peers:
        pl.semaphore_signal(
            barrier, inc=1, device_id=(peer // cond_size, peer % cond_size, grid),
            device_id_type=pl.DeviceIdType.MESH,
        )
    transform()
    pl.semaphore_wait(barrier, len(line_peers) + len(group_peers))

    def partial_copy(step, block):
        peer = (grid + step) % grid_size
        slot = (step - 1) * val_size + block
        return copy(
            part_ref.at[peer, block], inbox.at[step - 1, block], rs_send.at[slot],
            rs_recv.at[slot], (val, cond, peer),
        )

    def pick_remote(turn, first, last):
        def one(index, carry):
            step = index // cond_size + 1
            block = index % cond_size * blocks + turn
            pick((grid + step) % grid_size, block, part_ref)
            partial_copy(step, block).start()
            return carry

        lax.fori_loop(first, last, one, 0)

    def pick_own(turn):
        def one(index, carry):
            pick(grid, index * blocks + turn, part_ref)
            return carry

        lax.fori_loop(0, cond_size, one, 0)

    steps = [(0, step) for step in range(1, cond_size)] + [
        (around, step) for around in range(1, grid_size) for step in range(cond_size)
    ]

    def own_copy(turn, around, step):
        peer = (cond + step) % cond_size
        slot = (turn * grid_size + around) * cond_size + step
        return copy(
            own.at[peer * blocks + turn], columns_ref.at[grid, turn, val, cond],
            own_send.at[slot], own_recv.at[slot], (val, peer, (grid + around) % grid_size),
        )

    def row_copy(step, source):
        peer = (group + step) % group_size
        return copy(
            own.at[peer // cond_size], rows_ref.at[source // cond_size, source % cond_size],
            row_send.at[step], row_recv.at[step], (peer // cond_size, peer % cond_size, grid),
        )

    def reduce_own(turn):
        for part in range(cond_size):
            block = part * blocks + turn
            total = part_ref[grid, block].astype(jnp.float32)
            for step in range(1, grid_size):
                partial_copy(step, block).wait_recv()
                total = total + inbox[step - 1, block].astype(jnp.float32)
            own[block] = total.astype(own.dtype)
        columns_ref[grid, turn, val, cond] = own[cond * blocks + turn]
        for around, step in steps:
            own_copy(turn, around, step).start()

    def send_rows(turn):
        for step in range(1, group_size):

            @pl.when((group + step) % group_size // cond_size % blocks == turn)
            def start():
                row_copy(step, group).start()

    sent = []

    def piece_copy(turn, where, source_val, send, device):
        piece = columns_ref.at[where, turn, source_val]
        receive = piece_recv.at[(turn * val_size + source_val) * grid_size + where]
        return copy(piece, piece, send, receive, device)

    def start(piece):
        piece.start()
        sent.append(piece)

    def forward(turn, where, source_val, slot):
        send = core_send.at[turn * val_size * grid_size + slot]
        start(piece_copy(turn, where, source_val, send, (sibling, cond, grid)))

    def spread(turn, where, slot):
        for index, peer in enumerate(others):
            send = val_send.at[(turn * val_size + index) * grid_size + slot]
            start(piece_copy(turn, where, val, send, (peer, cond, grid)))
        forward(turn, where, val, slot)

    def arrive(turn, where, source_val):
        piece_copy(turn, where, source_val, core_send.at[0], (sibling, cond, grid)).wait_recv()

    def own_spread(turn, slot):
        around = (grid_size - order[slot]) % grid_size
        for step in range(0 if around else 1, cond_size):
            own_copy(turn, around, step).wait_recv()
        spread(turn, places[slot], slot)

    def pass_on(turn, slot):
        for index, peer in enumerate(others):
            arrive(turn, places[slot], peer)
            forward(turn, places[slot], peer, grid_size * (index + 1) + slot)

    tiles = cond_size * (grid_size - 1)
    for turn in range(blocks):
        if turn == 0:
            pick_remote(turn, 0, tiles)
        else:
            pick_remote(turn, 0, tiles // 3)
            reduce_own(turn - 1)
            send_rows(turn - 1)
            pick_remote(turn, tiles // 3, tiles * 2 // 3)
            own_spread(turn - 1, 0)
            pick_remote(turn, tiles * 2 // 3, tiles)
            for slot in range(1, grid_size - 1):
                own_spread(turn - 1, slot)
        pick_own(turn)
        if turn > 0:
            own_spread(turn - 1, grid_size - 1)
    reduce_own(blocks - 1)
    send_rows(blocks - 1)
    rows_ref[val, cond] = own[val]
    for turn in range(blocks - 1):
        for slot in range(grid_size):
            pass_on(turn, slot)
    own_spread(blocks - 1, 0)
    for slot in range(1, grid_size):
        own_spread(blocks - 1, slot)
        pass_on(blocks - 1, slot - 1)
    pass_on(blocks - 1, grid_size - 1)
    for turn in range(blocks):
        for where in places:
            for source in across:
                arrive(turn, where, source)
    for step in range(1, group_size):
        row_copy(step, (group + group_size - step) % group_size).wait_recv()
        row_copy(step, group).wait_send()
    for turn in range(blocks):
        for around, step in steps:
            own_copy(turn, around, step).wait_send()
    for step in range(1, grid_size):
        for block in range(val_size):
            partial_copy(step, block).wait_send()
    for piece in sent:
        piece.wait_send()


def response_kernel(bands, val_size, cond_size, valence_ref, conduction_ref, rows_ref, columns_ref, out_ref, left):
    depth = rows_ref.shape[0]
    width = rows_ref.shape[1]
    height = columns_ref.shape[-2]

    @pl.when((pl.program_id(0) == 0) & (pl.program_id(1) == 0))
    def scale_rows():
        row = lax.broadcasted_iota(jnp.int32, (depth, LANES), 0)
        group, pair = row // height, row % (height // 2)
        bands_other = height // 2 // bands
        valence_band = group // cond_size * bands + pair // bands_other
        conduction_band = group % cond_size * bands_other + pair % bands_other
        energy = jnp.zeros((depth, LANES), jnp.float32)
        for band in range(val_size * bands):
            energy = jnp.where(valence_band == band, valence_ref[band], energy)
        other = jnp.zeros((depth, LANES), jnp.float32)
        for band in range(cond_size * bands_other):
            other = jnp.where(conduction_band == band, conduction_ref[band], other)
        delta = energy - other
        weights = 4.0 * delta / (delta * delta + freq_squared) / math.sqrt(depth // 2)
        scaled = rows_ref[...].astype(jnp.float32) * weights[:, :1]
        pairs = scaled.reshape(-1, 2, height // 2, width)
        turned = jnp.concatenate([pairs[:, 1:], -pairs[:, :1]], axis=1).reshape(depth, width)
        left[:width] = scaled.T.astype(left.dtype)
        left[width:] = turned.T.astype(left.dtype)

    right = columns_ref[...].reshape(depth, columns_ref.shape[-1])
    out_ref[...] = jnp.dot(left[...], right, preferred_element_type=jnp.float32).reshape(
        out_ref.shape
    )


def response(valence_energy, conduction_energy, rows, columns):
    grid_size, blocks, val_size, cond_size, height, width = columns.shape
    depth = val_size * cond_size * height
    bands = valence_energy.shape[0] // val_size
    smem = pl.BlockSpec(memory_space=pltpu.SMEM)
    return pl.pallas_call(
        functools.partial(response_kernel, bands, val_size, cond_size),
        out_shape=jax.ShapeDtypeStruct((2, width, blocks * grid_size * width), jnp.float32),
        grid=(blocks, grid_size),
        in_specs=[
            smem,
            smem,
            pl.BlockSpec((depth, width), lambda block, place: (0, 0)),
            pl.BlockSpec(
                (None, None, val_size, cond_size, height, width),
                lambda block, place: (place, block, 0, 0, 0, 0),
            ),
        ],
        out_specs=pl.BlockSpec(
            (2, width, width), lambda block, place: (0, 0, block * grid_size + place)
        ),
        scratch_shapes=[pltpu.VMEM((2 * width, depth), jnp.bfloat16)],
        compiler_params=pltpu.CompilerParams(vmem_limit_bytes=60 * 2**20),
        name="response",
    )(valence_energy, conduction_energy, rows, columns)


def local(valence_orbitals, conduction_orbitals, valence_energy, conduction_energy, grid_index):
    valence_groups = lax.axis_size("val")
    conduction_groups = lax.axis_size("cond")
    grid_groups = lax.axis_size("grid")
    valence_local = valence_orbitals.shape[0]
    conduction_local = conduction_orbitals.shape[0]
    pair_count = valence_local * conduction_local
    vectors = grid_index.shape[0]
    row_width = vectors // (valence_groups * grid_groups)
    column_width = vectors // conduction_groups
    groups = valence_groups * conduction_groups
    depth = groups * 2 * pair_count

    remote = valence_groups % 2 == 0 and valence_groups % conduction_groups == 0
    remote = remote and grid_groups > 1
    result = partial_spectra(valence_orbitals, conduction_orbitals, grid_index, remote)
    if remote:
        columns, rows = result
        return response(
            valence_energy, conduction_energy, rows.reshape(depth, row_width), columns
        )

    delta = valence_energy[:, None] - conduction_energy[None, :]
    all_pairs = valence_energy.shape[0] * conduction_energy.shape[0]
    weights = 4.0 * delta / (delta * delta + freq_squared) / math.sqrt(all_pairs)
    weights = weights.reshape(valence_groups, valence_local, conduction_groups, conduction_local)
    weights = jnp.transpose(weights, (0, 2, 1, 3)).reshape(groups, 1, pair_count, 1)
    arrived = lax.all_to_all(result, "grid", split_axis=0, concat_axis=0, tiled=True)
    own = jnp.sum(arrived.astype(jnp.float32), axis=0).astype(jnp.bfloat16)
    everything = lax.all_gather(own, ("val", "cond"), axis=0, tiled=False)
    rows = lax.dynamic_index_in_dim(everything, lax.axis_index("val"), 1, keepdims=False)
    rows = rows.reshape(groups, 2, pair_count, row_width)
    columns = lax.all_gather(jnp.swapaxes(everything, 1, 2), "grid", axis=3, tiled=False)
    columns = lax.dynamic_slice_in_dim(
        columns.reshape(depth, vectors), lax.axis_index("cond") * column_width, column_width, 1
    )
    scaled = (rows.astype(jnp.float32) * weights).astype(jnp.bfloat16)
    turned = jnp.stack([scaled[:, 1], -scaled[:, 0]], axis=1)
    both = jnp.stack([scaled, turned], axis=0).reshape(2, depth, row_width)
    return lax.dot_general(
        both, columns, (((1,), (0,)), ((), ())), preferred_element_type=jnp.float32
    )


def solution(mesh):
    return jax.shard_map(
        local,
        mesh=mesh,
        in_specs=(P("val", "grid", None), P("cond", "grid", None), P(), P(), P()),
        out_specs=P(None, ("val", "grid"), "cond"),
        check_vma=False,
    )
```

```python
import functools
import math

import jax
import jax.numpy as jnp
import ml_dtypes
import numpy as np
from jax import lax
from jax.experimental import pallas as pl
from jax.experimental.pallas import tpu as pltpu
from jax.sharding import PartitionSpec as P

freq_squared = 4.0
LANES = 128
SUBLANES = 8
INPUTS = 9


def line_tables(points):
    indices = np.arange(points, dtype=np.int32)
    phases = indices[:, None] * indices[None, :] % points
    angles = phases.astype(np.float32) * np.float32(2.0 * math.pi / points)
    return (np.cos(angles).astype(ml_dtypes.bfloat16), (-np.sin(angles)).astype(ml_dtypes.bfloat16))


def spectra_steps(
    points, half, half_pad, bands, unroll, width,
    index_ref, valence_ref, conduction_ref, spread_ref, z_ref, y_ref, x_cos_ref, x_sin_ref,
    fold_ref, lines, planes, picked, cos_ref, sin_ref,
):
    parts = 2 * bands
    groups = points // SUBLANES
    pitch = SUBLANES + 1
    depth = valence_ref.shape[1]
    used = conduction_ref.shape[0] * depth
    line_bits = (2 * points - 1).bit_length()

    def fill(group):
        rows = pl.ds(pl.multiple_of(group * SUBLANES, SUBLANES), SUBLANES)
        cos_block = x_cos_ref[lax.axis_index("grid"), rows, :]
        sin_block = x_sin_ref[lax.axis_index("grid"), rows, :]
        upper = lax.broadcasted_iota(jnp.int32, (parts, LANES), 0) < bands
        for inner in range(SUBLANES):
            cos_row = jnp.broadcast_to(cos_block[inner : inner + 1], (parts, LANES))
            sin_row = jnp.broadcast_to(sin_block[inner : inner + 1], (parts, LANES))
            line = group * SUBLANES + inner
            cos_ref[line] = cos_row
            sin_ref[line] = jnp.where(upper, -sin_row, sin_row)
            cos_ref[points + line] = jnp.where(upper, cos_row, -cos_row)
            sin_ref[points + line] = -sin_row

    def z_pass(group):
        span = SUBLANES * points
        place = pl.ds(pl.multiple_of(group * span, LANES), span)
        valence = valence_ref[:, :, place].astype(jnp.float32).reshape(bands * depth, span)
        conduction = conduction_ref[:, :, place].astype(jnp.float32).reshape(used, span)
        if used < LANES:
            conduction = jnp.concatenate(
                [conduction, jnp.zeros((LANES - used, span), jnp.float32)], axis=0
            )
        wide = jnp.dot(
            valence.T.astype(jnp.bfloat16), spread_ref[...], preferred_element_type=jnp.float32
        )
        products = (wide * jnp.concatenate([conduction.T] * bands, axis=1)).astype(jnp.bfloat16)
        for inner in range(SUBLANES):
            result = jnp.dot(
                z_ref[...],
                products[inner * points : (inner + 1) * points],
                preferred_element_type=jnp.float32,
            )
            for part in range(parts):
                kind, band = part // bands, part % bands
                start = (part * groups + group) * half * pitch + inner
                lines[pl.ds(start, half, stride=pitch), :] = result[
                    kind * half_pad : kind * half_pad + half, band * LANES : (band + 1) * LANES
                ]

    def y_pass(q):
        def slab(part):
            return jnp.concatenate(
                [
                    lines[pl.ds(((part * groups + group) * half + q) * pitch, SUBLANES), :]
                    for group in range(groups)
                ],
                axis=0,
            )

        block = jnp.concatenate(
            [
                jnp.concatenate([slab(kind * bands + band) for band in range(bands)], axis=1)
                for kind in range(2)
            ],
            axis=0,
        ).astype(jnp.bfloat16)
        result = jnp.dot(y_ref[...], block, preferred_element_type=jnp.float32)
        for part in range(parts):
            kind, band = part // bands, part % bands
            planes[pl.ds(q * points * pitch + part, points, stride=pitch), :] = result[
                kind * points : (kind + 1) * points, band * LANES : (band + 1) * LANES
            ]

    def pick(place, block, out_ref):
        first = (block * out_ref.shape[0] + place) * width

        def some(step, carry):
            found = []
            for inner in range(unroll):
                vector = first + step * unroll + inner
                word = index_ref[vector]
                line = lax.bitwise_and(word, 2**line_bits - 1)
                row = lax.shift_right_logical(word, line_bits)
                values = planes[pl.ds(row, parts), :]
                swapped = pltpu.roll(values, bands, axis=0)
                found.append(values * cos_ref[line] + swapped * sin_ref[line])
            for inner in range(unroll):
                picked[pl.ds((step * unroll + inner) * pitch, parts), :] = found[inner]
            return carry

        lax.fori_loop(0, width // unroll, some, 0)
        rows = jnp.concatenate(
            [picked[pl.ds(part, width, stride=pitch), :].astype(jnp.bfloat16) for part in range(parts)],
            axis=1,
        )
        folded = jnp.dot(rows, fold_ref[...], preferred_element_type=jnp.float32)
        out_ref[place, block] = folded.T[: out_ref.shape[2], :].astype(out_ref.dtype)

    def loop(count, body, step):
        def several(index, carry):
            for inner in range(step):
                body(index * step + inner)
            return carry

        lax.fori_loop(0, count // step, several, 0)
        for rest in range(count - count % step, count):
            body(rest)

    def transform():
        loop(groups, fill, 1)
        loop(groups, z_pass, 1)
        loop(half, y_pass, 7)

    return transform, pick


def spectra_kernel(sizes, *refs):
    out_ref = refs[INPUTS]
    transform, pick = spectra_steps(*sizes, *refs[:INPUTS], *refs[INPUTS + 1 :])
    transform()

    def tile(index, carry):
        pick(index % out_ref.shape[0], index // out_ref.shape[0], out_ref)
        return carry

    lax.fori_loop(0, out_ref.shape[0] * out_ref.shape[1], tile, 0)


def partial_spectra(
    valence, conduction, valence_energy, conduction_energy, grid_index, remote
):
    valence_groups = lax.axis_size("val")
    grid_groups = lax.axis_size("grid")
    bands, depth, plane = valence.shape
    conduction_bands = conduction.shape[0]
    points = depth * lax.axis_size("grid")
    half = points // 2 + 1
    half_pad = -(-half // 16) * 16
    used = conduction_bands * depth
    parts = 2 * bands
    vectors = grid_index.shape[0]
    width = vectors // (grid_groups * valence_groups)
    line_cos, line_sin = line_tables(points)

    spread = np.zeros((bands * depth, bands, LANES), np.float32)
    for band in range(bands):
        for other in range(conduction_bands):
            for x in range(depth):
                spread[band * depth + x, band, other * depth + x] = 1.0
    spread = spread.reshape(bands * depth, bands * LANES).astype(ml_dtypes.bfloat16)
    columns = parts * conduction_bands
    fold = np.zeros((parts, LANES, LANES), np.float32)
    for part in range(parts):
        for other in range(conduction_bands):
            fold[part, other * depth : (other + 1) * depth, part * conduction_bands + other] = 1.0
    fold = fold.reshape(parts * LANES, LANES).astype(ml_dtypes.bfloat16)

    z_table = np.zeros((2 * half_pad, points), ml_dtypes.bfloat16)
    z_table[:half] = line_cos.T[:half]
    z_table[half_pad : half_pad + half] = line_sin.T[:half]
    y_table = np.concatenate(
        [
            np.concatenate([line_cos.T, -line_sin.T], axis=1),
            np.concatenate([line_sin.T, line_cos.T], axis=1),
        ],
        axis=0,
    )

    def lanes_of(table):
        lanes = np.zeros((grid_groups, points, LANES), np.float32)
        for place in range(grid_groups):
            own = table[place * depth : (place + 1) * depth].T.astype(np.float32)
            lanes[place, :, :used] = np.tile(own * np.float32(points ** (-1.5)), (1, conduction_bands))
        return lanes

    line = grid_index // (points * points)
    remainder = grid_index % (points * points)
    row = remainder // points
    column = remainder % points
    mirrored = column >= half
    line = jnp.where(mirrored, points + (points - line) % points, line)
    row = jnp.where(mirrored, (points - row) % points, row)
    column = jnp.where(mirrored, points - column, column)
    place = (column * points + row) * (SUBLANES + 1)
    index = place * 2 ** (2 * points - 1).bit_length() + line

    operands = (
        index, valence, conduction, spread, z_table, y_table, lanes_of(line_cos),
        lanes_of(line_sin), fold,
    )
    sizes = (points, half, half_pad, bands, 32, width)
    scratch = [
        pltpu.VMEM(
            ((parts * points // SUBLANES * half + SUBLANES) * (SUBLANES + 1), LANES), jnp.float32
        ),
        pltpu.VMEM((half * points * (SUBLANES + 1), LANES), jnp.float32),
        pltpu.VMEM((width * (SUBLANES + 1), LANES), jnp.float32),
        pltpu.VMEM((2 * points, parts, LANES), jnp.float32),
        pltpu.VMEM((2 * points, parts, LANES), jnp.float32),
    ]
    partial = (grid_groups, valence_groups, columns, width)
    vmem = pl.BlockSpec(memory_space=pltpu.VMEM)
    smem = pl.BlockSpec(memory_space=pltpu.SMEM)
    specs = [smem] + [vmem] * (INPUTS - 1)
    if not remote:
        return pl.pallas_call(
            functools.partial(spectra_kernel, sizes),
            out_shape=jax.ShapeDtypeStruct(partial, jnp.bfloat16),
            in_specs=specs,
            out_specs=vmem,
            scratch_shapes=scratch,
            compiler_params=pltpu.CompilerParams(vmem_limit_bytes=60 * 2**20),
            name="spectra",
        )(*operands)
    cond_groups = lax.axis_size("cond")
    blocks = valence_groups // cond_groups
    groups = valence_groups * cond_groups
    dma = pltpu.SemaphoreType.DMA
    return pl.pallas_call(
        functools.partial(exchange_kernel, sizes),
        out_shape=[
            jax.ShapeDtypeStruct(
                (grid_groups, blocks, valence_groups, cond_groups, columns, width), jnp.bfloat16
            ),
            jax.ShapeDtypeStruct((2 * width, groups * columns), jnp.bfloat16),
        ],
        in_specs=specs + [smem, smem],
        out_specs=[vmem, vmem],
        scratch_shapes=scratch
        + [
            pltpu.VMEM(partial, jnp.bfloat16),
            pltpu.VMEM((grid_groups - 1,) + partial[1:], jnp.bfloat16),
            pltpu.VMEM(partial[1:], jnp.bfloat16),
            pltpu.VMEM((valence_groups, cond_groups, columns, width), jnp.bfloat16),
            dma(((grid_groups - 1) * valence_groups,)),
            dma(((grid_groups - 1) * valence_groups,)),
            dma((groups,)),
            dma((groups,)),
            dma((blocks * cond_groups * grid_groups,)),
            dma((blocks * cond_groups * grid_groups,)),
            dma((blocks * valence_groups * grid_groups,)),
            dma((blocks * valence_groups * grid_groups,)),
            dma((blocks * valence_groups * grid_groups,)),
        ],
        compiler_params=pltpu.CompilerParams(
            collective_id=0, has_side_effects=True, vmem_limit_bytes=60 * 2**20
        ),
        name="spectra_exchange",
    )(*operands, valence_energy, conduction_energy)


def scale_rows(valence_ref, conduction_ref, rows_ref, left_ref):
    val_size, cond_size, height, width = rows_ref.shape
    depth = val_size * cond_size * height
    bands = valence_ref.shape[0] // val_size
    row = lax.broadcasted_iota(jnp.int32, (depth, LANES), 0)
    group, pair = row // height, row % (height // 2)
    bands_other = height // 2 // bands
    valence_band = group // cond_size * bands + pair // bands_other
    conduction_band = group % cond_size * bands_other + pair % bands_other
    energy = jnp.zeros((depth, LANES), jnp.float32)
    for band in range(val_size * bands):
        energy = jnp.where(valence_band == band, valence_ref[band], energy)
    other = jnp.zeros((depth, LANES), jnp.float32)
    for band in range(cond_size * bands_other):
        other = jnp.where(conduction_band == band, conduction_ref[band], other)
    delta = energy - other
    weights = 4.0 * delta / (delta * delta + freq_squared) / math.sqrt(depth // 2)
    scaled = rows_ref[...].reshape(depth, width).astype(jnp.float32) * weights[:, :1]
    pairs = scaled.reshape(-1, 2, height // 2, width)
    turned = jnp.concatenate([pairs[:, 1:], -pairs[:, :1]], axis=1).reshape(depth, width)
    left_ref[:width] = scaled.T.astype(left_ref.dtype)
    left_ref[width:] = turned.T.astype(left_ref.dtype)


def exchange_kernel(sizes, *refs):
    columns_ref, left_ref = refs[INPUTS + 2 : INPUTS + 4]
    part_ref, inbox, own, rows_ref = refs[INPUTS + 9 : INPUTS + 13]
    (
        rs_send, rs_recv, row_send, row_recv, own_send, own_recv, piece_recv, val_send, core_send,
    ) = refs[INPUTS + 13 :]
    transform, pick = spectra_steps(*sizes, *refs[:INPUTS], *refs[INPUTS + 4 : INPUTS + 9])
    val_size, cond_size, grid_size = (lax.axis_size(name) for name in ("val", "cond", "grid"))
    val, cond, grid = (lax.axis_index(name) for name in ("val", "cond", "grid"))
    blocks = val_size // cond_size
    group = val * cond_size + cond
    sibling = val + 1 - 2 * (val % 2)
    others = [(val + 2 * step) % val_size for step in range(1, val_size // 2)]
    across = [(sibling + 2 * step) % val_size for step in range(val_size // 2)]
    grid_peers = [(grid + step) % grid_size for step in range(1, grid_size)]
    group_size = val_size * cond_size
    group_peers = [(group + step) % group_size for step in range(1, group_size)]
    order = [0] + sorted(range(1, grid_size), key=lambda step: min(step, grid_size - step))
    places = [(grid + step) % grid_size for step in order]

    def copy(source, target, send, receive, device):
        return pltpu.make_async_remote_copy(
            src_ref=source, dst_ref=target, send_sem=send, recv_sem=receive, device_id=device,
            device_id_type=pl.DeviceIdType.MESH,
        )

    barrier = pltpu.get_barrier_semaphore()
    line_peers = [
        ((cond + step) % cond_size, peer) for step in range(cond_size) for peer in grid_peers
    ]
    for peer in line_peers:
        pl.semaphore_signal(
            barrier, inc=1, device_id=(val, *peer), device_id_type=pl.DeviceIdType.MESH
        )
    for peer in group_peers:
        pl.semaphore_signal(
            barrier, inc=1, device_id=(peer // cond_size, peer % cond_size, grid),
            device_id_type=pl.DeviceIdType.MESH,
        )
    transform()
    pl.semaphore_wait(barrier, len(line_peers) + len(group_peers))

    def partial_copy(step, block):
        peer = (grid + step) % grid_size
        slot = (step - 1) * val_size + block
        return copy(
            part_ref.at[peer, block], inbox.at[step - 1, block], rs_send.at[slot],
            rs_recv.at[slot], (val, cond, peer),
        )

    def pick_remote(turn, first, last):
        def one(index, carry):
            step = index // cond_size + 1
            block = index % cond_size * blocks + turn
            pick((grid + step) % grid_size, block, part_ref)
            partial_copy(step, block).start()
            return carry

        lax.fori_loop(first, last, one, 0)

    def pick_own(turn):
        def one(index, carry):
            pick(grid, index * blocks + turn, part_ref)
            return carry

        lax.fori_loop(0, cond_size, one, 0)

    steps = [(0, step) for step in range(1, cond_size)] + [
        (around, step) for around in range(1, grid_size) for step in range(cond_size)
    ]

    def own_copy(turn, around, step):
        peer = (cond + step) % cond_size
        slot = (turn * grid_size + around) * cond_size + step
        return copy(
            own.at[peer * blocks + turn], columns_ref.at[grid, turn, val, cond],
            own_send.at[slot], own_recv.at[slot], (val, peer, (grid + around) % grid_size),
        )

    def row_copy(step, source):
        peer = (group + step) % group_size
        return copy(
            own.at[peer // cond_size], rows_ref.at[source // cond_size, source % cond_size],
            row_send.at[step], row_recv.at[step], (peer // cond_size, peer % cond_size, grid),
        )

    def reduce_own(turn):
        for part in range(cond_size):
            block = part * blocks + turn
            total = part_ref[grid, block].astype(jnp.float32)
            for step in range(1, grid_size):
                partial_copy(step, block).wait_recv()
                total = total + inbox[step - 1, block].astype(jnp.float32)
            own[block] = total.astype(own.dtype)
        columns_ref[grid, turn, val, cond] = own[cond * blocks + turn]
        for around, step in steps:
            own_copy(turn, around, step).start()

    def send_rows(turn):
        for step in range(1, group_size):

            @pl.when((group + step) % group_size // cond_size % blocks == turn)
            def start():
                row_copy(step, group).start()

    sent = []

    def piece_copy(turn, where, source_val, send, device):
        piece = columns_ref.at[where, turn, source_val]
        receive = piece_recv.at[(turn * val_size + source_val) * grid_size + where]
        return copy(piece, piece, send, receive, device)

    def start(piece):
        piece.start()
        sent.append(piece)

    def forward(turn, where, source_val, slot):
        send = core_send.at[turn * val_size * grid_size + slot]
        start(piece_copy(turn, where, source_val, send, (sibling, cond, grid)))

    def spread(turn, where, slot):
        for index, peer in enumerate(others):
            send = val_send.at[(turn * val_size + index) * grid_size + slot]
            start(piece_copy(turn, where, val, send, (peer, cond, grid)))
        forward(turn, where, val, slot)

    def arrive(turn, where, source_val):
        piece_copy(turn, where, source_val, core_send.at[0], (sibling, cond, grid)).wait_recv()

    def own_spread(turn, slot):
        around = (grid_size - order[slot]) % grid_size
        for step in range(0 if around else 1, cond_size):
            own_copy(turn, around, step).wait_recv()
        spread(turn, places[slot], slot)

    def pass_on(turn, slot):
        for index, peer in enumerate(others):
            arrive(turn, places[slot], peer)
            forward(turn, places[slot], peer, grid_size * (index + 1) + slot)

    tiles = cond_size * (grid_size - 1)
    for turn in range(blocks):
        if turn == 0:
            pick_remote(turn, 0, tiles)
        else:
            pick_remote(turn, 0, tiles // 3)
            reduce_own(turn - 1)
            send_rows(turn - 1)
            pick_remote(turn, tiles // 3, tiles * 2 // 3)
            own_spread(turn - 1, 0)
            pick_remote(turn, tiles * 2 // 3, tiles)
            for slot in range(1, grid_size - 1):
                own_spread(turn - 1, slot)
        pick_own(turn)
        if turn > 0:
            own_spread(turn - 1, grid_size - 1)
    reduce_own(blocks - 1)
    send_rows(blocks - 1)
    rows_ref[val, cond] = own[val]
    for turn in range(blocks - 2):
        for slot in range(grid_size):
            pass_on(turn, slot)
    for slot in range(grid_size):
        if blocks > 1:
            pass_on(blocks - 2, slot)
        own_spread(blocks - 1, slot)
    for step in range(1, group_size):
        row_copy(step, (group + group_size - step) % group_size).wait_recv()
    pass_on(blocks - 1, 0)
    scale_rows(*refs[INPUTS : INPUTS + 2], rows_ref, left_ref)
    for slot in range(1, grid_size):
        pass_on(blocks - 1, slot)
    for turn in range(blocks):
        for where in places:
            for source in across:
                arrive(turn, where, source)
    for step in range(1, group_size):
        row_copy(step, group).wait_send()
    for turn in range(blocks):
        for around, step in steps:
            own_copy(turn, around, step).wait_send()
    for step in range(1, grid_size):
        for block in range(val_size):
            partial_copy(step, block).wait_send()
    for piece in sent:
        piece.wait_send()


def response_kernel(left_ref, columns_ref, out_ref):
    depth = left_ref.shape[1]
    right = columns_ref[...].reshape(depth, columns_ref.shape[-1])
    out_ref[...] = jnp.dot(left_ref[...], right, preferred_element_type=jnp.float32).reshape(
        out_ref.shape
    )


def response(left, columns):
    grid_size, blocks, val_size, cond_size, height, width = columns.shape
    depth = val_size * cond_size * height
    return pl.pallas_call(
        response_kernel,
        out_shape=jax.ShapeDtypeStruct((2, width, blocks * grid_size * width), jnp.float32),
        grid=(blocks, grid_size),
        in_specs=[
            pl.BlockSpec((2 * width, depth), lambda block, place: (0, 0)),
            pl.BlockSpec(
                (None, None, val_size, cond_size, height, width),
                lambda block, place: (place, block, 0, 0, 0, 0),
            ),
        ],
        out_specs=pl.BlockSpec(
            (2, width, width), lambda block, place: (0, 0, block * grid_size + place)
        ),
        compiler_params=pltpu.CompilerParams(vmem_limit_bytes=60 * 2**20),
        name="response",
    )(left, columns)


def local(valence_orbitals, conduction_orbitals, valence_energy, conduction_energy, grid_index):
    valence_groups = lax.axis_size("val")
    conduction_groups = lax.axis_size("cond")
    grid_groups = lax.axis_size("grid")
    valence_local = valence_orbitals.shape[0]
    conduction_local = conduction_orbitals.shape[0]
    pair_count = valence_local * conduction_local
    vectors = grid_index.shape[0]
    row_width = vectors // (valence_groups * grid_groups)
    column_width = vectors // conduction_groups
    groups = valence_groups * conduction_groups
    depth = groups * 2 * pair_count

    remote = valence_groups % 2 == 0 and valence_groups % conduction_groups == 0
    remote = remote and grid_groups > 1
    result = partial_spectra(
        valence_orbitals, conduction_orbitals, valence_energy, conduction_energy, grid_index, remote
    )
    if remote:
        columns, left = result
        return response(left, columns)

    delta = valence_energy[:, None] - conduction_energy[None, :]
    all_pairs = valence_energy.shape[0] * conduction_energy.shape[0]
    weights = 4.0 * delta / (delta * delta + freq_squared) / math.sqrt(all_pairs)
    weights = weights.reshape(valence_groups, valence_local, conduction_groups, conduction_local)
    weights = jnp.transpose(weights, (0, 2, 1, 3)).reshape(groups, 1, pair_count, 1)
    arrived = lax.all_to_all(result, "grid", split_axis=0, concat_axis=0, tiled=True)
    own = jnp.sum(arrived.astype(jnp.float32), axis=0).astype(jnp.bfloat16)
    everything = lax.all_gather(own, ("val", "cond"), axis=0, tiled=False)
    rows = lax.dynamic_index_in_dim(everything, lax.axis_index("val"), 1, keepdims=False)
    rows = rows.reshape(groups, 2, pair_count, row_width)
    columns = lax.all_gather(jnp.swapaxes(everything, 1, 2), "grid", axis=3, tiled=False)
    columns = lax.dynamic_slice_in_dim(
        columns.reshape(depth, vectors), lax.axis_index("cond") * column_width, column_width, 1
    )
    scaled = (rows.astype(jnp.float32) * weights).astype(jnp.bfloat16)
    turned = jnp.stack([scaled[:, 1], -scaled[:, 0]], axis=1)
    both = jnp.stack([scaled, turned], axis=0).reshape(2, depth, row_width)
    return lax.dot_general(
        both, columns, (((1,), (0,)), ((), ())), preferred_element_type=jnp.float32
    )


def solution(mesh):
    return jax.shard_map(
        local,
        mesh=mesh,
        in_specs=(P("val", "grid", None), P("cond", "grid", None), P(), P(), P()),
        out_specs=P(None, ("val", "grid"), "cond"),
        check_vma=False,
    )
```

```python
import functools
import math

import jax
import jax.numpy as jnp
import ml_dtypes
import numpy as np
from jax import lax
from jax.experimental import pallas as pl
from jax.experimental.pallas import tpu as pltpu
from jax.sharding import PartitionSpec as P

freq_squared = 4.0
LANES = 128
SUBLANES = 8
INPUTS = 9


def line_tables(points):
    indices = np.arange(points, dtype=np.int32)
    phases = indices[:, None] * indices[None, :] % points
    angles = phases.astype(np.float32) * np.float32(2.0 * math.pi / points)
    return (np.cos(angles).astype(ml_dtypes.bfloat16), (-np.sin(angles)).astype(ml_dtypes.bfloat16))


def spectra_steps(
    points, half, half_pad, bands, unroll, width,
    index_ref, valence_ref, conduction_ref, spread_ref, z_ref, y_ref, x_cos_ref, x_sin_ref,
    fold_ref, lines, planes, picked, cos_ref, sin_ref,
):
    parts = 2 * bands
    groups = points // SUBLANES
    pitch = SUBLANES + 1
    depth = valence_ref.shape[1]
    used = conduction_ref.shape[0] * depth
    line_bits = (2 * points - 1).bit_length()

    def fill(group):
        rows = pl.ds(pl.multiple_of(group * SUBLANES, SUBLANES), SUBLANES)
        cos_block = x_cos_ref[lax.axis_index("grid"), rows, :]
        sin_block = x_sin_ref[lax.axis_index("grid"), rows, :]
        upper = lax.broadcasted_iota(jnp.int32, (parts, LANES), 0) < bands
        for inner in range(SUBLANES):
            cos_row = jnp.broadcast_to(cos_block[inner : inner + 1], (parts, LANES))
            sin_row = jnp.broadcast_to(sin_block[inner : inner + 1], (parts, LANES))
            line = group * SUBLANES + inner
            cos_ref[line] = cos_row
            sin_ref[line] = jnp.where(upper, -sin_row, sin_row)
            cos_ref[points + line] = jnp.where(upper, cos_row, -cos_row)
            sin_ref[points + line] = -sin_row

    def z_pass(group):
        span = SUBLANES * points
        place = pl.ds(pl.multiple_of(group * span, LANES), span)
        valence = valence_ref[:, :, place].astype(jnp.float32).reshape(bands * depth, span)
        conduction = conduction_ref[:, :, place].astype(jnp.float32).reshape(used, span)
        if used < LANES:
            conduction = jnp.concatenate(
                [conduction, jnp.zeros((LANES - used, span), jnp.float32)], axis=0
            )
        wide = jnp.dot(
            valence.T.astype(jnp.bfloat16), spread_ref[...], preferred_element_type=jnp.float32
        )
        products = (wide * jnp.concatenate([conduction.T] * bands, axis=1)).astype(jnp.bfloat16)
        for inner in range(SUBLANES):
            result = jnp.dot(
                z_ref[...],
                products[inner * points : (inner + 1) * points],
                preferred_element_type=jnp.float32,
            )
            for part in range(parts):
                kind, band = part // bands, part % bands
                start = (part * groups + group) * half * pitch + inner
                lines[pl.ds(start, half, stride=pitch), :] = result[
                    kind * half_pad : kind * half_pad + half, band * LANES : (band + 1) * LANES
                ]

    def y_pass(q):
        def slab(part):
            return jnp.concatenate(
                [
                    lines[pl.ds(((part * groups + group) * half + q) * pitch, SUBLANES), :]
                    for group in range(groups)
                ],
                axis=0,
            )

        block = jnp.concatenate(
            [
                jnp.concatenate([slab(kind * bands + band) for band in range(bands)], axis=1)
                for kind in range(2)
            ],
            axis=0,
        ).astype(jnp.bfloat16)
        result = jnp.dot(y_ref[...], block, preferred_element_type=jnp.float32)
        for part in range(parts):
            kind, band = part // bands, part % bands
            planes[pl.ds(q * points * pitch + part, points, stride=pitch), :] = result[
                kind * points : (kind + 1) * points, band * LANES : (band + 1) * LANES
            ]

    def pick(place, block, out_ref):
        first = (block * out_ref.shape[0] + place) * width

        def some(step, carry):
            found = []
            for inner in range(unroll):
                vector = first + step * unroll + inner
                word = index_ref[vector]
                line = lax.bitwise_and(word, 2**line_bits - 1)
                row = lax.shift_right_logical(word, line_bits)
                values = planes[pl.ds(row, parts), :]
                swapped = pltpu.roll(values, bands, axis=0)
                found.append(values * cos_ref[line] + swapped * sin_ref[line])
            for inner in range(unroll):
                picked[pl.ds((step * unroll + inner) * pitch, parts), :] = found[inner]
            return carry

        lax.fori_loop(0, width // unroll, some, 0)
        rows = jnp.concatenate(
            [picked[pl.ds(part, width, stride=pitch), :].astype(jnp.bfloat16) for part in range(parts)],
            axis=1,
        )
        folded = jnp.dot(rows, fold_ref[...], preferred_element_type=jnp.float32)
        out_ref[place, block] = folded.T[: out_ref.shape[2], :].astype(out_ref.dtype)

    def loop(count, body, step):
        def several(index, carry):
            for inner in range(step):
                body(index * step + inner)
            return carry

        lax.fori_loop(0, count // step, several, 0)
        for rest in range(count - count % step, count):
            body(rest)

    def transform():
        loop(groups, fill, 1)
        loop(groups, z_pass, 1)
        loop(half, y_pass, 7)

    return transform, pick


def spectra_kernel(sizes, *refs):
    out_ref = refs[INPUTS]
    transform, pick = spectra_steps(*sizes, *refs[:INPUTS], *refs[INPUTS + 1 :])
    transform()

    def tile(index, carry):
        pick(index % out_ref.shape[0], index // out_ref.shape[0], out_ref)
        return carry

    lax.fori_loop(0, out_ref.shape[0] * out_ref.shape[1], tile, 0)


def partial_spectra(
    valence, conduction, valence_energy, conduction_energy, grid_index, remote
):
    valence_groups = lax.axis_size("val")
    grid_groups = lax.axis_size("grid")
    bands, depth, plane = valence.shape
    conduction_bands = conduction.shape[0]
    points = depth * lax.axis_size("grid")
    half = points // 2 + 1
    half_pad = -(-half // 16) * 16
    used = conduction_bands * depth
    parts = 2 * bands
    vectors = grid_index.shape[0]
    width = vectors // (grid_groups * valence_groups)
    line_cos, line_sin = line_tables(points)

    spread = np.zeros((bands * depth, bands, LANES), np.float32)
    for band in range(bands):
        for other in range(conduction_bands):
            for x in range(depth):
                spread[band * depth + x, band, other * depth + x] = 1.0
    spread = spread.reshape(bands * depth, bands * LANES).astype(ml_dtypes.bfloat16)
    columns = parts * conduction_bands
    fold = np.zeros((parts, LANES, LANES), np.float32)
    for part in range(parts):
        for other in range(conduction_bands):
            fold[part, other * depth : (other + 1) * depth, part * conduction_bands + other] = 1.0
    fold = fold.reshape(parts * LANES, LANES).astype(ml_dtypes.bfloat16)

    z_table = np.zeros((2 * half_pad, points), ml_dtypes.bfloat16)
    z_table[:half] = line_cos.T[:half]
    z_table[half_pad : half_pad + half] = line_sin.T[:half]
    y_table = np.concatenate(
        [
            np.concatenate([line_cos.T, -line_sin.T], axis=1),
            np.concatenate([line_sin.T, line_cos.T], axis=1),
        ],
        axis=0,
    )

    def lanes_of(table):
        lanes = np.zeros((grid_groups, points, LANES), np.float32)
        for place in range(grid_groups):
            own = table[place * depth : (place + 1) * depth].T.astype(np.float32)
            lanes[place, :, :used] = np.tile(own * np.float32(points ** (-1.5)), (1, conduction_bands))
        return lanes

    line = grid_index // (points * points)
    remainder = grid_index % (points * points)
    row = remainder // points
    column = remainder % points
    mirrored = column >= half
    line = jnp.where(mirrored, points + (points - line) % points, line)
    row = jnp.where(mirrored, (points - row) % points, row)
    column = jnp.where(mirrored, points - column, column)
    place = (column * points + row) * (SUBLANES + 1)
    index = place * 2 ** (2 * points - 1).bit_length() + line

    operands = (
        index, valence, conduction, spread, z_table, y_table, lanes_of(line_cos),
        lanes_of(line_sin), fold,
    )
    sizes = (points, half, half_pad, bands, 32, width)
    scratch = [
        pltpu.VMEM(
            ((parts * points // SUBLANES * half + SUBLANES) * (SUBLANES + 1), LANES), jnp.float32
        ),
        pltpu.VMEM((half * points * (SUBLANES + 1), LANES), jnp.float32),
        pltpu.VMEM((width * (SUBLANES + 1), LANES), jnp.float32),
        pltpu.VMEM((2 * points, parts, LANES), jnp.float32),
        pltpu.VMEM((2 * points, parts, LANES), jnp.float32),
    ]
    partial = (grid_groups, valence_groups, columns, width)
    vmem = pl.BlockSpec(memory_space=pltpu.VMEM)
    smem = pl.BlockSpec(memory_space=pltpu.SMEM)
    specs = [smem] + [vmem] * (INPUTS - 1)
    if not remote:
        return pl.pallas_call(
            functools.partial(spectra_kernel, sizes),
            out_shape=jax.ShapeDtypeStruct(partial, jnp.bfloat16),
            in_specs=specs,
            out_specs=vmem,
            scratch_shapes=scratch,
            compiler_params=pltpu.CompilerParams(vmem_limit_bytes=60 * 2**20),
            name="spectra",
        )(*operands)
    cond_groups = lax.axis_size("cond")
    blocks = valence_groups // cond_groups
    groups = valence_groups * cond_groups
    dma = pltpu.SemaphoreType.DMA
    return pl.pallas_call(
        functools.partial(exchange_kernel, sizes),
        out_shape=[
            jax.ShapeDtypeStruct(
                (grid_groups, blocks, valence_groups, cond_groups, columns, width), jnp.bfloat16
            ),
            jax.ShapeDtypeStruct((2 * width, groups * columns), jnp.bfloat16),
        ],
        in_specs=specs + [smem, smem],
        out_specs=[vmem, vmem],
        scratch_shapes=scratch
        + [
            pltpu.VMEM(partial, jnp.bfloat16),
            pltpu.VMEM((grid_groups - 1,) + partial[1:], jnp.bfloat16),
            pltpu.VMEM(partial[1:], jnp.bfloat16),
            pltpu.VMEM((valence_groups, cond_groups, columns, width), jnp.bfloat16),
            dma(((grid_groups - 1) * valence_groups,)),
            dma(((grid_groups - 1) * valence_groups,)),
            dma((groups,)),
            dma((groups,)),
            dma((blocks * cond_groups * grid_groups,)),
            dma((blocks * cond_groups * grid_groups,)),
            dma((blocks * valence_groups * grid_groups,)),
            dma((blocks * valence_groups * grid_groups,)),
            dma((blocks * valence_groups * grid_groups,)),
        ],
        compiler_params=pltpu.CompilerParams(
            collective_id=0, has_side_effects=True, vmem_limit_bytes=60 * 2**20
        ),
        name="spectra_exchange",
    )(*operands, valence_energy, conduction_energy)


def scale_rows(valence_ref, conduction_ref, rows_ref, left_ref):
    val_size, cond_size, height, width = rows_ref.shape
    depth = val_size * cond_size * height
    bands = valence_ref.shape[0] // val_size
    row = lax.broadcasted_iota(jnp.int32, (depth, LANES), 0)
    group, pair = row // height, row % (height // 2)
    bands_other = height // 2 // bands
    valence_band = group // cond_size * bands + pair // bands_other
    conduction_band = group % cond_size * bands_other + pair % bands_other
    energy = jnp.zeros((depth, LANES), jnp.float32)
    for band in range(val_size * bands):
        energy = jnp.where(valence_band == band, valence_ref[band], energy)
    other = jnp.zeros((depth, LANES), jnp.float32)
    for band in range(cond_size * bands_other):
        other = jnp.where(conduction_band == band, conduction_ref[band], other)
    delta = energy - other
    weights = 4.0 * delta / (delta * delta + freq_squared) / math.sqrt(depth // 2)
    scaled = rows_ref[...].reshape(depth, width).astype(jnp.float32) * weights[:, :1]
    pairs = scaled.reshape(-1, 2, height // 2, width)
    turned = jnp.concatenate([pairs[:, 1:], -pairs[:, :1]], axis=1).reshape(depth, width)
    left_ref[:width] = scaled.T.astype(left_ref.dtype)
    left_ref[width:] = turned.T.astype(left_ref.dtype)


def exchange_kernel(sizes, *refs):
    columns_ref, left_ref = refs[INPUTS + 2 : INPUTS + 4]
    part_ref, inbox, own, rows_ref = refs[INPUTS + 9 : INPUTS + 13]
    (
        rs_send, rs_recv, row_send, row_recv, own_send, own_recv, piece_recv, val_send, core_send,
    ) = refs[INPUTS + 13 :]
    transform, pick = spectra_steps(*sizes, *refs[:INPUTS], *refs[INPUTS + 4 : INPUTS + 9])
    val_size, cond_size, grid_size = (lax.axis_size(name) for name in ("val", "cond", "grid"))
    val, cond, grid = (lax.axis_index(name) for name in ("val", "cond", "grid"))
    blocks = val_size // cond_size
    group = val * cond_size + cond
    sibling = val + 1 - 2 * (val % 2)
    others = [(val + 2 * step) % val_size for step in range(1, val_size // 2)]
    across = [(sibling + 2 * step) % val_size for step in range(val_size // 2)]
    grid_peers = [(grid + step) % grid_size for step in range(1, grid_size)]
    group_size = val_size * cond_size
    group_peers = [(group + step) % group_size for step in range(1, group_size)]
    order = [0] + sorted(range(1, grid_size), key=lambda step: min(step, grid_size - step))
    places = [(grid + step) % grid_size for step in order]

    def copy(source, target, send, receive, device):
        return pltpu.make_async_remote_copy(
            src_ref=source, dst_ref=target, send_sem=send, recv_sem=receive, device_id=device,
            device_id_type=pl.DeviceIdType.MESH,
        )

    barrier = pltpu.get_barrier_semaphore()
    line_peers = [
        ((cond + step) % cond_size, peer) for step in range(cond_size) for peer in grid_peers
    ]
    for peer in line_peers:
        pl.semaphore_signal(
            barrier, inc=1, device_id=(val, *peer), device_id_type=pl.DeviceIdType.MESH
        )
    for peer in group_peers:
        pl.semaphore_signal(
            barrier, inc=1, device_id=(peer // cond_size, peer % cond_size, grid),
            device_id_type=pl.DeviceIdType.MESH,
        )
    transform()
    pl.semaphore_wait(barrier, len(line_peers) + len(group_peers))

    def partial_copy(step, block):
        peer = (grid + step) % grid_size
        slot = (step - 1) * val_size + block
        return copy(
            part_ref.at[peer, block], inbox.at[step - 1, block], rs_send.at[slot],
            rs_recv.at[slot], (val, cond, peer),
        )

    def pick_remote(turn, first, last):
        def one(index, carry):
            step = index // cond_size + 1
            block = index % cond_size * blocks + turn
            pick((grid + step) % grid_size, block, part_ref)
            partial_copy(step, block).start()
            return carry

        lax.fori_loop(first, last, one, 0)

    def pick_own(turn):
        def one(index, carry):
            pick(grid, index * blocks + turn, part_ref)
            return carry

        lax.fori_loop(0, cond_size, one, 0)

    steps = [(0, step) for step in range(1, cond_size)] + [
        (around, step) for around in range(1, grid_size) for step in range(cond_size)
    ]

    def own_copy(turn, around, step):
        peer = (cond + step) % cond_size
        slot = (turn * grid_size + around) * cond_size + step
        return copy(
            own.at[peer * blocks + turn], columns_ref.at[grid, turn, val, cond],
            own_send.at[slot], own_recv.at[slot], (val, peer, (grid + around) % grid_size),
        )

    def row_copy(step, source):
        peer = (group + step) % group_size
        return copy(
            own.at[peer // cond_size], rows_ref.at[source // cond_size, source % cond_size],
            row_send.at[step], row_recv.at[step], (peer // cond_size, peer % cond_size, grid),
        )

    def reduce_own(turn):
        for part in range(cond_size):
            block = part * blocks + turn
            total = part_ref[grid, block].astype(jnp.float32)
            for step in range(1, grid_size):
                partial_copy(step, block).wait_recv()
                total = total + inbox[step - 1, block].astype(jnp.float32)
            own[block] = total.astype(own.dtype)
        columns_ref[grid, turn, val, cond] = own[cond * blocks + turn]
        for around, step in steps:
            own_copy(turn, around, step).start()

    def send_rows(turn):
        for step in range(1, group_size):

            @pl.when((group + step) % group_size // cond_size % blocks == turn)
            def start():
                row_copy(step, group).start()

    sent = []

    def piece_copy(turn, where, source_val, send, device):
        piece = columns_ref.at[where, turn, source_val]
        receive = piece_recv.at[(turn * val_size + source_val) * grid_size + where]
        return copy(piece, piece, send, receive, device)

    def start(piece):
        piece.start()
        sent.append(piece)

    def forward(turn, where, source_val, slot):
        send = core_send.at[turn * val_size * grid_size + slot]
        start(piece_copy(turn, where, source_val, send, (sibling, cond, grid)))

    def spread(turn, where, slot):
        for index, peer in enumerate(others):
            send = val_send.at[(turn * val_size + index) * grid_size + slot]
            start(piece_copy(turn, where, val, send, (peer, cond, grid)))
        forward(turn, where, val, slot)

    def arrive(turn, where, source_val):
        piece_copy(turn, where, source_val, core_send.at[0], (sibling, cond, grid)).wait_recv()

    def own_spread(turn, slot):
        around = (grid_size - order[slot]) % grid_size
        for step in range(0 if around else 1, cond_size):
            own_copy(turn, around, step).wait_recv()
        spread(turn, places[slot], slot)

    def pass_on(turn, slot):
        for index, peer in enumerate(others):
            arrive(turn, places[slot], peer)
            forward(turn, places[slot], peer, grid_size * (index + 1) + slot)

    tiles = cond_size * (grid_size - 1)
    for turn in range(blocks):
        if turn == 0:
            pick_remote(turn, 0, tiles)
        else:
            pick_remote(turn, 0, tiles // 3)
            reduce_own(turn - 1)
            send_rows(turn - 1)
            pick_remote(turn, tiles // 3, tiles * 2 // 3)
            own_spread(turn - 1, 0)
            pick_remote(turn, tiles * 2 // 3, tiles)
            for slot in range(1, grid_size - 1):
                own_spread(turn - 1, slot)
        pick_own(turn)
        if turn > 0:
            own_spread(turn - 1, grid_size - 1)
    reduce_own(blocks - 1)
    send_rows(blocks - 1)
    rows_ref[val, cond] = own[val]
    for turn in range(blocks - 2):
        for slot in range(grid_size):
            pass_on(turn, slot)
    for slot in range(grid_size):
        if blocks > 1:
            pass_on(blocks - 2, slot)
        own_spread(blocks - 1, slot)
    for step in range(1, group_size):
        row_copy(step, (group + group_size - step) % group_size).wait_recv()
    pass_on(blocks - 1, 0)
    scale_rows(*refs[INPUTS : INPUTS + 2], rows_ref, left_ref)
    for slot in range(1, grid_size):
        pass_on(blocks - 1, slot)
    for turn in range(blocks):
        for where in places:
            for source in across:
                arrive(turn, where, source)
    for step in range(1, group_size):
        row_copy(step, group).wait_send()
    for turn in range(blocks):
        for around, step in steps:
            own_copy(turn, around, step).wait_send()
    for step in range(1, grid_size):
        for block in range(val_size):
            partial_copy(step, block).wait_send()
    for piece in sent:
        piece.wait_send()


def response_kernel(left_ref, columns_ref, out_ref):
    depth = left_ref.shape[1]
    width = columns_ref.shape[-1]
    right = jnp.concatenate(
        [columns_ref[place].reshape(depth, width) for place in range(columns_ref.shape[0])], axis=1
    )
    out_ref[...] = jnp.dot(left_ref[...], right, preferred_element_type=jnp.float32).reshape(
        out_ref.shape
    )


def response(left, columns):
    grid_size, blocks, val_size, cond_size, height, width = columns.shape
    depth = val_size * cond_size * height
    joined = 2 if grid_size % 2 == 0 else 1
    return pl.pallas_call(
        response_kernel,
        out_shape=jax.ShapeDtypeStruct((2, width, blocks * grid_size * width), jnp.float32),
        grid=(blocks, grid_size // joined),
        in_specs=[
            pl.BlockSpec((2 * width, depth), lambda block, place: (0, 0)),
            pl.BlockSpec(
                (joined, None, val_size, cond_size, height, width),
                lambda block, place: (place, block, 0, 0, 0, 0),
            ),
        ],
        out_specs=pl.BlockSpec(
            (2, width, joined * width),
            lambda block, place: (0, 0, block * (grid_size // joined) + place),
        ),
        compiler_params=pltpu.CompilerParams(vmem_limit_bytes=60 * 2**20),
        name="response",
    )(left, columns)


def local(valence_orbitals, conduction_orbitals, valence_energy, conduction_energy, grid_index):
    valence_groups = lax.axis_size("val")
    conduction_groups = lax.axis_size("cond")
    grid_groups = lax.axis_size("grid")
    valence_local = valence_orbitals.shape[0]
    conduction_local = conduction_orbitals.shape[0]
    pair_count = valence_local * conduction_local
    vectors = grid_index.shape[0]
    row_width = vectors // (valence_groups * grid_groups)
    column_width = vectors // conduction_groups
    groups = valence_groups * conduction_groups
    depth = groups * 2 * pair_count

    remote = valence_groups % 2 == 0 and valence_groups % conduction_groups == 0
    remote = remote and grid_groups > 1
    result = partial_spectra(
        valence_orbitals, conduction_orbitals, valence_energy, conduction_energy, grid_index, remote
    )
    if remote:
        columns, left = result
        return response(left, columns)

    delta = valence_energy[:, None] - conduction_energy[None, :]
    all_pairs = valence_energy.shape[0] * conduction_energy.shape[0]
    weights = 4.0 * delta / (delta * delta + freq_squared) / math.sqrt(all_pairs)
    weights = weights.reshape(valence_groups, valence_local, conduction_groups, conduction_local)
    weights = jnp.transpose(weights, (0, 2, 1, 3)).reshape(groups, 1, pair_count, 1)
    arrived = lax.all_to_all(result, "grid", split_axis=0, concat_axis=0, tiled=True)
    own = jnp.sum(arrived.astype(jnp.float32), axis=0).astype(jnp.bfloat16)
    everything = lax.all_gather(own, ("val", "cond"), axis=0, tiled=False)
    rows = lax.dynamic_index_in_dim(everything, lax.axis_index("val"), 1, keepdims=False)
    rows = rows.reshape(groups, 2, pair_count, row_width)
    columns = lax.all_gather(jnp.swapaxes(everything, 1, 2), "grid", axis=3, tiled=False)
    columns = lax.dynamic_slice_in_dim(
        columns.reshape(depth, vectors), lax.axis_index("cond") * column_width, column_width, 1
    )
    scaled = (rows.astype(jnp.float32) * weights).astype(jnp.bfloat16)
    turned = jnp.stack([scaled[:, 1], -scaled[:, 0]], axis=1)
    both = jnp.stack([scaled, turned], axis=0).reshape(2, depth, row_width)
    return lax.dot_general(
        both, columns, (((1,), (0,)), ((), ())), preferred_element_type=jnp.float32
    )


def solution(mesh):
    return jax.shard_map(
        local,
        mesh=mesh,
        in_specs=(P("val", "grid", None), P("cond", "grid", None), P(), P(), P()),
        out_specs=P(None, ("val", "grid"), "cond"),
        check_vma=False,
    )
```
